32 devices in a mesh: member: 8 (over y, x, core), tile: 4 (over z).
Axes of the slice: x: 2, y: 2, z: 4, core: 2. Of those that a mesh axis runs over, the one named last changes fastest.
Arguments:
- atmos_state: float32 [8, 4, 32, 72, 256], P('member', None, 'tile'), may hold values from -6 to 6
- ocean_slots: float32 [8, 4, 32, 62, 256], P('member', None, 'tile'), may hold values from -6 to 6
- owner_map: int32 [4], P('tile'), may hold values from 0 to 7
- land_mask: int32 [32, 256], P('tile'), may hold values 0 or 1
- transfer_coefficient: float32 [32, 256], P('tile'), may hold values from 0.5 to 2
- air_mixing: float32 [72, 72], replicated, may hold values from -0.75 to 0.75
- sea_mixing: float32 [62, 62], replicated, may hold values from -0.75 to 0.75
Outputs:
- atmos_next: float32 [8, 4, 32, 72, 256], P('member', None, 'tile')
- ocean_next: float32 [8, 4, 32, 62, 256], P('member', None, 'tile')
The draws below stay inside these ranges and needn't reach their ends.
Inputs may be any that keep to these rules, and one draw needn't show every extreme that they name: owner_map[t] is the member whose slot holds tile t's ocean; the other slots of that tile are not read.
All inputs are finite; a program needn't handle non-finite values. No bound on the sum of `land_mask` on one device may be relied on, other than what follows from the above.
Results may differ from the reference program's by a relative error of at most 0.0001.
Values sent between devices are 32-bit elements; how exact they have to be, the bound alone decides.
No kernel may reach another device: no remote copies, remote signals or barrier semaphores. Data moves between devices by JAX's collectives and lax.ppermute only.
A program may use at most 64 MiB of HBM per device.

```python
import math
import jax
import jax.numpy as jnp
from jax import lax

LEV = 72
OLEV = 62
ROWS = 8
NLON = 256
NSUB = 4
MEMBERS = 8
NTILES = 4
NLAT = 32


def place_ends(entries, stream_key, low, high):
    place = [jax.random.randint(jax.random.fold_in(stream_key, axis), (), 0, length) for axis, length in enumerate(entries.shape)]
    main_axis = entries.shape.index(max(entries.shape))
    beside = place[:main_axis] + [(place[main_axis] + 1) % entries.shape[main_axis]] + place[main_axis + 1:]
    return entries.at[tuple(place)].set(low).at[tuple(beside)].set(high)


def block_levels(key, shape, cuts, least, largest):
    level, own = 1.0, jax.random.fold_in(key, 6)
    for position, blocks in cuts:
        steps = jnp.exp(jax.random.uniform(jax.random.fold_in(own, position), (blocks,), jnp.float32, least / len(cuts), largest / len(cuts)))
        level = level * jnp.repeat(steps, shape[position] // blocks).reshape([-1 if axis == position else 1 for axis in range(len(shape))])
    return level


def gaussian(stream_key, shape, deviation, reach, shards=(), held_as=jnp.bfloat16):
    values = jax.random.normal(stream_key, shape, jnp.float32) * deviation
    if len(shards) > 0:
        values = block_levels(stream_key, shape, shards, -0.22, 0.18) * values
    return jnp.clip(values, min=-reach, max=reach).astype(held_as)


def setup_inputs(seed: int = 0) -> dict:
    key_list = jax.random.split(jax.random.key(seed), 8)
    atmos_state = gaussian(key_list[0], (MEMBERS, 4, NLAT, LEV, NLON), 1.0, 6.0, ((0, 8), (2, 4)), jnp.float32)
    ocean_slots = gaussian(key_list[1], (MEMBERS, 4, NLAT, OLEV, NLON), 1.0, 6.0, ((0, 8), (2, 4)), jnp.float32)
    owner_map = place_ends(jax.random.randint(key_list[2], (NTILES,), 0, MEMBERS), jax.random.fold_in(key_list[2], 1), 0, MEMBERS - 1).astype(jnp.int32)
    land_mask = place_ends((jax.random.randint(key_list[3], (NLAT, NLON), 0, 10) < 7).astype(jnp.int32), jax.random.fold_in(key_list[3], 1), 0, 1)
    transfer_coefficient = jnp.clip(jnp.exp(math.log(2.0) - 1.3862944 * jax.random.uniform(key_list[4], (NLAT, NLON), jnp.float32) ** block_levels(key_list[4], (NLAT, NLON), ((0, 4),), -0.2, 0.2)), 0.5, 2.0)
    air_mixing = gaussian(key_list[5], (LEV, LEV), LEV ** -0.5, 0.75, (), jnp.float32)
    sea_mixing = gaussian(key_list[6], (OLEV, OLEV), OLEV ** -0.5, 0.75, (), jnp.float32)
    return dict(atmos_state=atmos_state, ocean_slots=ocean_slots, owner_map=owner_map, land_mask=land_mask, transfer_coefficient=transfer_coefficient, air_mixing=air_mixing, sea_mixing=sea_mixing)


DIFFUSE = 0.2
ADVECT_RATE = 0.15
CORIOLIS_MAX = 0.2
AIR_STEP = 0.05
SEA_STEP = 0.25

def coriolis_of(row_index, row_total):
    latitude = math.pi * ((row_index.astype(jnp.float32) + 0.5) / row_total - 0.5)
    return (CORIOLIS_MAX * jnp.sin(latitude)).reshape(-1, 1, 1)

def dynamics(padded, coriolis):
    center = padded[:, 1:-1]
    north_row = padded[:, 2:]
    south_row = padded[:, :-2]
    east_col = jnp.roll(center, -1, axis=3)
    west_col = jnp.roll(center, 1, axis=3)
    laplace = north_row + south_row + east_col + west_col - 4.0 * center
    zonal_diff = 0.5 * (east_col - west_col)
    merid_diff = 0.5 * (north_row - south_row)
    east_wind = center[2]
    north_wind = center[3]
    advect = east_wind * zonal_diff[:2] + north_wind * merid_diff[:2]
    tracers = center[:2] + DIFFUSE * laplace[:2] - ADVECT_RATE * advect
    east_new = east_wind + DIFFUSE * laplace[2] + coriolis * north_wind
    north_new = north_wind + DIFFUSE * laplace[3] - coriolis * east_wind
    return jnp.concatenate([tracers, east_new[None], north_new[None]], axis=0)

def column_mix(fields, mixing):
    moved = jnp.einsum('kl,frlc->frkc', mixing, fields, precision=lax.Precision.HIGHEST)
    return 0.5 * fields + 0.5 * moved

def fluxes(fields, surface):
    east_diff = fields[2, :, 0, :] - surface[1]
    north_diff = fields[3, :, 0, :] - surface[2]
    speed = jnp.sqrt(1.0 + east_diff * east_diff + north_diff * north_diff)
    factor = surface[3] * speed
    return jnp.stack([factor * (surface[0] - fields[0, :, 0, :]), factor * (jnp.tanh(surface[0]) - fields[1, :, 0, :]), factor * east_diff, factor * north_diff])

def window(atmosphere, surface, air_mixing):
    coriolis = coriolis_of(jnp.arange(NLAT), NLAT)
    signs = jnp.array([1.0, 1.0, -1.0, -1.0], jnp.float32)[:, None, None]
    accumulated = jnp.zeros((4, NLAT, NLON), jnp.float32)
    for substep in range(NSUB):
        surface_flux = fluxes(atmosphere, surface)
        padded = jnp.pad(atmosphere, ((0, 0), (1, 1), (0, 0), (0, 0)))
        updated = column_mix(dynamics(padded, coriolis), air_mixing)
        atmosphere = updated.at[:, :, 0, :].add(AIR_STEP * signs * surface_flux)
        accumulated = accumulated + surface_flux
    return (atmosphere, accumulated / NSUB)

def reference(atmos_state, ocean_slots, owner_map, land_mask, transfer_coefficient, air_mixing, sea_mixing):
    owner_row = jnp.repeat(owner_map, ROWS, total_repeat_length=NLAT)
    is_owner = jnp.arange(MEMBERS)[:, None] == owner_row[None, :]
    ocean_block = lax.optimization_barrier(jnp.sum(jnp.where(is_owner[:, None, :, None, None], ocean_slots, 0.0), axis=0))
    weight = transfer_coefficient * land_mask.astype(jnp.float32)
    surface = jnp.stack([ocean_block[0, :, 0, :], ocean_block[2, :, 0, :], ocean_block[3, :, 0, :], weight])
    atmos_next, accumulated = jax.vmap(window, in_axes=(0, None, None))(atmos_state, surface, air_mixing)
    mean_flux = lax.optimization_barrier(jnp.sum(accumulated, axis=0)) / MEMBERS
    forced = ocean_block.at[:, :, 0, :].add(SEA_STEP * mean_flux)
    mixed_ocean = column_mix(forced, sea_mixing)
    stepped = jnp.where(land_mask[None, :, None, :] == 1, mixed_ocean, ocean_block)
    ocean_next = jnp.where(is_owner[:, None, :, None, None], stepped[None], ocean_slots)
    return (atmos_next, ocean_next)
```

```python
import functools
import math

import jax
import jax.numpy as jnp
from jax import lax
from jax.experimental import pallas as pl
from jax.experimental.pallas import tpu as pltpu
from jax.sharding import PartitionSpec as P

NSUB = 4
DIFFUSE = 0.2
ADVECT_RATE = 0.15
CORIOLIS_MAX = 0.2
AIR_STEP = 0.05
SEA_STEP = 0.25
SIGNS = (1.0, 1.0, -1.0, -1.0)
FIELDS = 4

F32 = jnp.float32
BF16 = jnp.bfloat16
AXES = ("member", "tile")
VMEM = pl.BlockSpec(memory_space=pltpu.VMEM)
SMEM = pl.BlockSpec(memory_space=pltpu.SMEM)
ANY = pl.BlockSpec(memory_space=pl.ANY)
VMEM_LIMIT = 12 * 2**20


def ceil_to(count, unit):
    return -(-count // unit) * unit


def split_parts(values):
    high = values.astype(BF16).astype(F32)
    return high, (values - high).astype(BF16).astype(F32)


def mixing_parts(mixing, scale):
    levels = mixing.shape[0]
    rows = lax.broadcasted_iota(jnp.int32, mixing.shape, 0)
    columns = lax.broadcasted_iota(jnp.int32, mixing.shape, 1)
    both = scale * mixing + jnp.where(rows == columns, scale, 0.0)
    high, low = split_parts(both)
    pad = jnp.zeros((levels, ceil_to(levels, 16) - levels), F32)
    parts = [high, pad, high, pad, low, pad]
    if pad.shape[1] == 0:
        parts = [high, high, low]
    return jnp.concatenate(parts, axis=1).astype(BF16)


def stage(cells, staged, offset, depth):
    count, lon = cells.shape
    if count < 16:
        cells = jnp.concatenate([cells, jnp.zeros((16 - count, lon), F32)], axis=0)
    high = cells.astype(BF16)
    low = (cells - high.astype(F32)).astype(BF16)
    staged[offset : offset + 16] = high
    staged[depth + offset : depth + offset + 16] = low
    staged[2 * depth + offset : 2 * depth + offset + 16] = high


def stage_dynamics(center, outer, inner, sign, coriolis, staged):
    levels, lon = center.shape[1:]
    depth = ceil_to(levels, 16)
    rate = 0.5 * ADVECT_RATE / DIFFUSE
    for offset in range(0, levels, 16):
        part = slice(offset, min(offset + 16, levels))
        cells = [center[f, part] for f in range(FIELDS)]
        east_wind = rate * cells[2]
        north_wind = (rate * sign) * cells[3]
        for f in range(FIELDS):
            outer_row, inner_row = outer[f, part], inner[f, part]
            east = pltpu.roll(cells[f], lon - 1, 1)
            west = pltpu.roll(cells[f], 1, 1)
            total = ((east + west) + (outer_row + inner_row)) + cells[f]
            if f < 2:
                total = total - (east_wind * (east - west) + north_wind * (outer_row - inner_row))
            elif f == 2:
                total = total + coriolis * cells[3]
            else:
                total = total - coriolis * cells[2]
            stage(total, staged.at[f], offset, depth)


def surface_flux(center, surface, place):
    sst, sst_tanh, cur_east, cur_north, rate = [surface[k, place] for k in range(5)]
    east = center[2, 0:1] - cur_east
    north = center[3, 0:1] - cur_north
    factor = rate * jnp.sqrt(1.0 + east * east + north * north)
    return (
        factor * (sst - center[0, 0:1]),
        factor * (sst_tanh - center[1, 0:1]),
        factor * east,
        factor * north,
    )


def tile_state(rows):
    tile = lax.axis_index("tile")
    return lax.rem(tile, 2) == 0, tile * rows


def own_row(north_first, rows, place):
    return jnp.where(north_first, rows - 1 - place, place)


def place_values(coriolis, rows, place):
    north_first, first_row = tile_state(rows)
    index = first_row + own_row(north_first, rows, place - NSUB)
    total = coriolis.shape[0] - 2 * NSUB
    valid = jnp.where((index >= 0) & (index < total), 1.0, 0.0)
    return coriolis[index + NSUB], valid


def advance(state, surface, total, weights, staged, coriolis, step, places, targets):
    rows = state.shape[1] - 2 * NSUB
    sign = jnp.where(tile_state(rows)[0], 1.0, -1.0)
    for k, place in enumerate(places):
        center, outer, inner = [state.at[step, place + shift] for shift in (0, -1, 1)]
        turn, _ = place_values(coriolis, rows, place)
        stage_dynamics(center, outer, inner, sign, turn, staged.at[k])
    for k, place in enumerate(places):
        center = state.at[step, place]
        target = targets[k]
        flux = surface_flux(center, surface, place)
        _, valid = place_values(coriolis, rows, place)
        for f in range(FIELDS):
            total[place, f] = total[place, f] + flux[f]
            mixed = jnp.dot(weights[...], staged[k, f], preferred_element_type=F32)
            target[f] = valid * mixed
            target[f, 0:1] = valid * (mixed[0:1] + (AIR_STEP * SIGNS[f]) * flux[f])


def pack_kernel(depth, owner, air, sea, first, second, top, sems, top_sems):
    rows = air.shape[2]
    north_first, _ = tile_state(rows)
    copies = []
    for d in range(depth):
        for side, out in enumerate((first, second)):
            row = own_row(north_first, rows, d if side == 0 else rows - 1 - d)
            copies.append(
                pltpu.make_async_copy(air.at[0, :, row], out.at[d], sems.at[2 * d + side])
            )
    for k, f in enumerate((0, 2, 3)):
        copies.append(pltpu.make_async_copy(sea.at[0, f, 0], top.at[k], top_sems.at[k]))
    for copy in copies:
        copy.start()
    for copy in copies:
        copy.wait()

    @pl.when(lax.axis_index("member") != owner[0])
    def _():
        top[...] = jnp.zeros_like(top)


def ocean_kernel(owner, air, sea, land, air_mixing, sea_mixing, state, weights, base, sea_next,
                 staged, sea_weights, sems, sea_sem):
    rows = air.shape[2]
    levels = sea.shape[2]
    depth = ceil_to(levels, 16)
    north_first, _ = tile_state(rows)
    copies = []
    for place in range(rows):
        row = own_row(north_first, rows, place)
        copies.append(
            pltpu.make_async_copy(air.at[0, :, row], state.at[0, NSUB + place], sems.at[place])
        )
    for copy in copies:
        copy.start()
    weights[...] = mixing_parts(air_mixing[...], 0.5 * DIFFUSE)

    @pl.when(lax.axis_index("member") == owner[0])
    def _():
        copy = pltpu.make_async_copy(sea.at[0], base, sea_sem)
        copy.start()
        sea_weights[...] = mixing_parts(sea_mixing[...], 0.5)
        copy.wait()

        def body(row, carry):
            for f in range(FIELDS):
                cells = base[f, :, row]
                for offset in range(0, levels, 16):
                    part = slice(offset, min(offset + 16, levels))
                    stage(cells[part], staged.at[f], offset, depth)
            at_sea = land[pl.ds(row, 1)] == 1
            for f in range(FIELDS):
                mixed = jnp.dot(sea_weights[...], staged[f], preferred_element_type=F32)
                base[f, :, row] = jnp.where(at_sea, mixed, base[f, :, row])
            return carry

        lax.fori_loop(0, rows, body, 0)

    @pl.when(lax.axis_index("member") != owner[0])
    def _():
        copy = pltpu.make_async_copy(sea, sea_next, sea_sem)
        copy.start()
        copy.wait()

    for copy in copies:
        copy.wait()


def interior_kernel(coriolis, top_a, top_b, top_c, top_d, land, transfer, weights, state_in,
                    state, surface, total, first, second, first_top, second_top, staged, sems):
    del state_in
    rows = land.shape[0]
    last = NSUB + rows - 1
    north_first, _ = tile_state(rows)
    copies = [
        pltpu.make_async_copy(state.at[0, NSUB + 2], first.at[0], sems.at[0]),
        pltpu.make_async_copy(state.at[0, last - 2], second.at[0], sems.at[1]),
    ]
    for copy in copies:
        copy.start()
    total[...] = jnp.zeros_like(total)
    for place in range(rows):
        row = pl.ds(own_row(north_first, rows, place), 1)
        for k, kept in enumerate((0, 2, 3)):
            value = (top_a[k, row] + top_b[k, row]) + (top_c[k, row] + top_d[k, row])
            surface[kept, NSUB + place] = value
        surface[1, NSUB + place] = jnp.tanh(surface[0, NSUB + place])
        surface[4, NSUB + place] = transfer[row] * land[row].astype(F32)
    for d in range(NSUB - 1):
        for k, kept in enumerate((0, 2, 3, 4)):
            first_top[k, d : d + 1] = surface[kept, NSUB + d]
            second_top[k, d : d + 1] = surface[kept, last - d]

    for step in range(NSUB - 1):
        def body(d, carry):
            places = (NSUB + d, last - d)
            targets = [state.at[step + 1, place] for place in places]
            advance(state, surface, total, weights, staged, coriolis, step, places, targets)
            return carry

        lax.fori_loop(step + 1, rows // 2, body, 0)
    for copy in copies:
        copy.wait()


def chain(number, state, surface, total, weights, staged, coriolis, final, arrived, arrived_at):
    places = state.shape[1]
    for side in range(2):
        place = NSUB - number if side == 0 else places - 1 - NSUB + number
        _, valid = place_values(coriolis, places - 2 * NSUB, place)
        for f in range(FIELDS):
            state[0, place, f] = valid * arrived[side][arrived_at, f]

    def step_places(step):
        low = NSUB + step + 1 - number
        return low, places - 1 - low

    def body(step, carry):
        pair = step_places(step)
        targets = [state.at[step + 1, place] for place in pair]
        advance(state, surface, total, weights, staged, coriolis, step, pair, targets)
        return carry

    lax.fori_loop(0, NSUB - 1, body, 0)
    pair = step_places(NSUB - 1)
    targets = [final.at[side] for side in range(2)]
    advance(state, surface, total, weights, staged, coriolis, NSUB - 1, pair, targets)


def send_rows(number, final, air_next, sems):
    rows = air_next.shape[2]
    north_first, _ = tile_state(rows)
    copies = []
    for side in range(2):
        row = own_row(north_first, rows, NSUB - number if side == 0 else rows - 1 - NSUB + number)
        copies.append(pltpu.make_async_copy(final.at[side], air_next.at[0, :, row], sems.at[side]))
    for copy in copies:
        copy.start()
    return copies


def halo_surface(surface, beside):
    places = surface.shape[1]
    for side in range(2):
        for d in range(NSUB - 1):
            place = NSUB - 1 - d if side == 0 else places - NSUB + d
            for k, kept in enumerate((0, 2, 3, 4)):
                surface[kept, place] = beside[side][k, d : d + 1]
            surface[1, place] = jnp.tanh(surface[0, place])


def first_chains_kernel(coriolis, weights, near, far, near_surface, far_surface,
                        state_in, surface_in, total_in, state, surface, total, air_next,
                        first, second, staged, final, sems, send_sems):
    del state_in, surface_in, total_in
    places = state.shape[1]
    sends = [
        pltpu.make_async_copy(state.at[0, NSUB + 3], first.at[0], send_sems.at[0]),
        pltpu.make_async_copy(state.at[0, places - 1 - NSUB - 3], second.at[0], send_sems.at[1]),
    ]
    for copy in sends:
        copy.start()
    halo_surface(surface, (near_surface, far_surface))
    copies = []
    for number in (1, 2):
        chain(number, state, surface, total, weights, staged, coriolis,
              final.at[number - 1], (near, far), number - 1)
        copies += send_rows(number, final.at[number - 1], air_next, sems.at[number - 1])
    for copy in sends + copies:
        copy.wait()


def third_chain_kernel(coriolis, weights, near, far, surface, state_in, total_in, air_in,
                       state, total, air_next, flux, staged, final, sems):
    del state_in, total_in, air_in
    rows = state.shape[1] - 2 * NSUB
    chain(3, state, surface, total, weights, staged, coriolis, final, (near, far), 0)
    copies = send_rows(3, final, air_next, sems)
    for place in (NSUB, NSUB + rows - 1):
        last = surface_flux(state.at[NSUB - 1, place], surface, place)
        for f in range(FIELDS):
            total[place, f] = total[place, f] + last[f]
    for place in range(rows):
        for f in range(FIELDS):
            flux[f, place : place + 1] = total[NSUB + place, f]
    for copy in copies:
        copy.wait()


def last_chain_kernel(coriolis, weights, near, far, surface, state_in, total_in, air_in,
                      air_next, state, total, staged, final, sems):
    del state_in, total_in, air_in
    chain(4, state, surface, total, weights, staged, coriolis, final, (near, far), 0)
    for copy in send_rows(4, final, air_next, sems):
        copy.wait()


def sea_kernel(scale, owner, column, flux_a, flux_b, flux_c, flux_d, land, base, sea_in, after,
               sea_next, result, mean, sems):
    del sea_in, after

    @pl.when(lax.axis_index("member") == owner[0])
    def _():
        rows, levels = land.shape[0], base.shape[1]
        north_first, _ = tile_state(rows)
        at_sea = land[...] == 1
        for f in range(FIELDS):
            for place in range(rows):
                part = slice(place, place + 1)
                value = (flux_a[f, part] + flux_b[f, part]) + (flux_c[f, part] + flux_d[f, part])
                mean[f, pl.ds(own_row(north_first, rows, place), 1)] = value
        copies = []
        for f in range(FIELDS):
            forcing = jnp.where(at_sea, (0.5 * scale) * mean[f], 0.0)
            for level in range(levels):
                factor = column[level] + 1.0 if level == 0 else column[level]
                result[f, level] = base[f, level] + factor * forcing
            copies.append(pltpu.make_async_copy(result.at[f], sea_next.at[0, f], sems.at[f]))
            copies[-1].start()
        for copy in copies:
            copy.wait()


def pairings(members, tiles):
    both = []
    for side in range(2):
        pairs = []
        for member in range(members):
            for tile in range(tiles):
                other = tile + 1 if (tile + side) % 2 == 0 else tile - 1
                if 0 <= other < tiles:
                    to = member * tiles + other
                else:
                    to = (member ^ 1) * tiles + tile
                pairs.append((member * tiles + tile, to))
        both.append(pairs)
    return both


def params(**more):
    return pltpu.CompilerParams(vmem_limit_bytes=VMEM_LIMIT, **more)


def cost(flops, moved):
    return pl.CostEstimate(flops=int(flops), bytes_accessed=int(moved), transcendentals=0)


def exchange(values, swaps):
    return [lax.ppermute(value, AXES, swap) for value, swap in zip(values, swaps)]


def member_parts(values, members):
    def swapped(block, k):
        return lax.ppermute(block, "member", [(i, i ^ k) for i in range(members)])

    k = 1
    while members > 4 * k:
        values = values + swapped(values, k)
        k *= 2
    parts = [values]
    for other in range(k, members, k):
        parts.append(swapped(values, other))
    return parts


def shards(
    atmos_state, ocean_slots, owner_map, land_mask, transfer_coefficient, air_mixing, sea_mixing
):
    members, tiles = lax.axis_size("member"), lax.axis_size("tile")
    _, _, rows, levels, lon = atmos_state.shape
    sea_levels = ocean_slots.shape[3]
    places = rows + 2 * NSUB
    depth, sea_depth = ceil_to(levels, 16), ceil_to(sea_levels, 16)
    swaps = pairings(members, tiles)
    sea_slots = jnp.swapaxes(ocean_slots, 2, 3)

    row_total = rows * tiles
    row_index = jnp.arange(-NSUB, row_total + NSUB)
    latitude = math.pi * ((row_index.astype(F32) + 0.5) / row_total - 0.5)
    coriolis = (CORIOLIS_MAX / DIFFUSE) * jnp.sin(latitude)

    def rows_of(count):
        return jax.ShapeDtypeStruct((count, FIELDS, levels, lon), F32)

    state_type = pltpu.VMEM((NSUB, places, FIELDS, levels, lon), F32)
    surface_type = pltpu.VMEM((5, places, 1, lon), F32)
    total_type = pltpu.VMEM((places, FIELDS, 1, lon), F32)
    staged = pltpu.VMEM((2, FIELDS, 3 * depth, lon), BF16)
    final = pltpu.VMEM((2, FIELDS, levels, lon), F32)
    air_type = pltpu.HBM(atmos_state.shape, F32)
    sea_type = pltpu.HBM(sea_slots.shape, F32)
    top_type = pltpu.VMEM((4, NSUB - 1, lon), F32)
    atmos_state = pltpu.with_memory_space_constraint(atmos_state, pltpu.HBM)
    sea_slots = pltpu.with_memory_space_constraint(sea_slots, pltpu.HBM)

    *near_rows, sea_top = pl.pallas_call(
        functools.partial(pack_kernel, 2),
        name="pack_rows",
        out_shape=(rows_of(2), rows_of(2), pltpu.VMEM((3, rows, lon), F32)),
        in_specs=[SMEM, ANY, ANY],
        out_specs=(ANY, ANY, VMEM),
        scratch_shapes=[pltpu.SemaphoreType.DMA((4,)), pltpu.SemaphoreType.DMA((3,))],
        compiler_params=params(),
    )(owner_map, atmos_state, sea_slots)
    arrived = exchange(near_rows, swaps)
    top_parts = member_parts(sea_top, members)

    state, weights, base, sea_next = pl.pallas_call(
        ocean_kernel,
        name="sea_mixing",
        out_shape=(
            state_type,
            pltpu.VMEM((levels, 3 * depth), BF16),
            pltpu.VMEM(sea_slots.shape[1:], F32),
            sea_type,
        ),
        in_specs=[SMEM, ANY, ANY, VMEM, VMEM, VMEM],
        out_specs=(VMEM, VMEM, VMEM, ANY),
        scratch_shapes=[
            pltpu.VMEM((FIELDS, 3 * sea_depth, lon), BF16),
            pltpu.VMEM((sea_levels, 3 * sea_depth), BF16),
            pltpu.SemaphoreType.DMA((rows,)),
            pltpu.SemaphoreType.DMA,
        ],
        compiler_params=params(),
    )(owner_map, atmos_state, sea_slots, land_mask, air_mixing, sea_mixing)

    state, surface, total, *more = pl.pallas_call(
        interior_kernel,
        name="interior",
        out_shape=(
            state_type, surface_type, total_type, rows_of(1), rows_of(1), top_type, top_type
        ),
        in_specs=[SMEM] + [VMEM] * 8,
        out_specs=(VMEM, VMEM, VMEM, ANY, ANY, VMEM, VMEM),
        input_output_aliases={8: 0},
        scratch_shapes=[staged, pltpu.SemaphoreType.DMA((2,))],
        compiler_params=params(),
    )(coriolis, *top_parts, land_mask, transfer_coefficient, weights, state)
    beside = exchange(more[2:], swaps)
    arrived_third = exchange(more[:2], swaps)

    state, surface, total, air_next, *fourth_rows = pl.pallas_call(
        first_chains_kernel,
        name="first_chains",
        out_shape=(state_type, surface_type, total_type, air_type, rows_of(1), rows_of(1)),
        in_specs=[SMEM] + [VMEM] * 8,
        out_specs=(VMEM, VMEM, VMEM, ANY, ANY, ANY),
        input_output_aliases={6: 0, 7: 1, 8: 2},
        scratch_shapes=[
            staged,
            pltpu.VMEM((2, 2, FIELDS, levels, lon), F32),
            pltpu.SemaphoreType.DMA((2, 2)),
            pltpu.SemaphoreType.DMA((2,)),
        ],
        compiler_params=params(),
    )(coriolis, weights, *arrived, *beside, state, surface, total)
    arrived_fourth = exchange(fourth_rows, swaps)

    state, total, air_next, flux = pl.pallas_call(
        third_chain_kernel,
        name="third_chain",
        out_shape=(state_type, total_type, air_type, pltpu.VMEM((FIELDS, rows, lon), F32)),
        in_specs=[SMEM] + [VMEM] * 6 + [ANY],
        out_specs=(VMEM, VMEM, ANY, VMEM),
        input_output_aliases={5: 0, 6: 1, 7: 2},
        scratch_shapes=[staged, final, pltpu.SemaphoreType.DMA((2,))],
        compiler_params=params(),
    )(coriolis, weights, *arrived_third, surface, state, total, air_next)
    flux_parts = member_parts(flux, members)

    air_next, _, _ = pl.pallas_call(
        last_chain_kernel,
        name="last_chain",
        out_shape=(air_type, state_type, total_type),
        in_specs=[SMEM] + [VMEM] * 6 + [ANY],
        out_specs=(ANY, VMEM, VMEM),
        input_output_aliases={5: 1, 6: 2, 7: 0},
        scratch_shapes=[staged, final, pltpu.SemaphoreType.DMA((2,))],
        compiler_params=params(),
    )(coriolis, weights, *arrived_fourth, surface, state, total, air_next)

    after = pltpu.with_memory_space_constraint(air_next, pltpu.HBM)
    sea_next = pl.pallas_call(
        functools.partial(sea_kernel, SEA_STEP / (NSUB * members)),
        name="sea_step",
        out_shape=sea_type,
        in_specs=[SMEM, SMEM] + [VMEM] * 6 + [ANY, ANY],
        out_specs=ANY,
        input_output_aliases={8: 0},
        scratch_shapes=[
            pltpu.VMEM(sea_slots.shape[1:], F32),
            pltpu.VMEM((FIELDS, rows, lon), F32),
            pltpu.SemaphoreType.DMA((FIELDS,)),
        ],
        compiler_params=params(),
    )(owner_map, sea_mixing[:, 0], *flux_parts, land_mask, base, sea_next, after)
    return (air_next, jnp.swapaxes(sea_next, 2, 3))


def solution(mesh):
    placed = (
        P("member", None, "tile", None, None),
        P("member", None, "tile", None, None),
        P("tile"),
        P("tile", None),
        P("tile", None),
        P(),
        P(),
    )
    return jax.shard_map(
        shards,
        mesh=mesh,
        in_specs=placed,
        out_specs=(P("member", None, "tile", None, None), P("member", None, "tile", None, None)),
        check_vma=False,
    )
```

```python
import functools
import math

import jax
import jax.numpy as jnp
from jax import lax
from jax.experimental import pallas as pl
from jax.experimental.pallas import tpu as pltpu
from jax.sharding import PartitionSpec as P

NSUB = 4
DIFFUSE = 0.2
ADVECT_RATE = 0.15
CORIOLIS_MAX = 0.2
AIR_STEP = 0.05
SEA_STEP = 0.25
SIGNS = (1.0, 1.0, -1.0, -1.0)
FIELDS = 4
LANES = 128

F32 = jnp.float32
BF16 = jnp.bfloat16
AXES = ("member", "tile")
VMEM = pl.BlockSpec(memory_space=pltpu.VMEM)
SMEM = pl.BlockSpec(memory_space=pltpu.SMEM)
ANY = pl.BlockSpec(memory_space=pl.ANY)
VMEM_LIMIT = 12 * 2**20


def ceil_to(count, unit):
    return -(-count // unit) * unit


def split_parts(values):
    high = values.astype(BF16).astype(F32)
    return high, (values - high).astype(BF16).astype(F32)


def mixing_parts(mixing, scale):
    levels = mixing.shape[0]
    rows = lax.broadcasted_iota(jnp.int32, mixing.shape, 0)
    columns = lax.broadcasted_iota(jnp.int32, mixing.shape, 1)
    both = scale * mixing + jnp.where(rows == columns, scale, 0.0)
    extra = ceil_to(levels, 8) - levels
    if extra:
        both = jnp.concatenate([both, jnp.zeros((extra, levels), F32)], axis=0)
    high, low = split_parts(both)
    pad = jnp.zeros((both.shape[0], ceil_to(levels, 16) - levels), F32)
    parts = [high, pad, high, pad, low, pad] if pad.shape[1] else [high, high, low]
    return jnp.concatenate(parts, axis=1).astype(BF16)


def stage(cells, staged, offset, depth):
    count, lon = cells.shape
    if count < 16:
        cells = jnp.concatenate([cells, jnp.zeros((16 - count, lon), F32)], axis=0)
    high = cells.astype(BF16)
    low = (cells - high.astype(F32)).astype(BF16)
    staged[offset : offset + 16] = high
    staged[depth + offset : depth + offset + 16] = low
    staged[2 * depth + offset : 2 * depth + offset + 16] = high


def stage_dynamics(center, outer, inner, sign, coriolis, staged):
    levels, lon = center.shape[1:]
    depth = ceil_to(levels, 16)
    rate = 0.5 * ADVECT_RATE / DIFFUSE
    for offset in range(0, levels, 16):
        part = slice(offset, min(offset + 16, levels))
        cells = [center[f, part] for f in range(FIELDS)]
        east_wind = rate * cells[2]
        north_wind = (rate * sign) * cells[3]
        for f in range(FIELDS):
            outer_row, inner_row = outer[f, part], inner[f, part]
            east = pltpu.roll(cells[f], lon - 1, 1)
            west = pltpu.roll(cells[f], 1, 1)
            total = ((east + west) + (outer_row + inner_row)) + cells[f]
            if f < 2:
                total = total - (east_wind * (east - west) + north_wind * (outer_row - inner_row))
            elif f == 2:
                total = total + coriolis * cells[3]
            else:
                total = total - coriolis * cells[2]
            stage(total, staged.at[f], offset, depth)


def surface_flux(center, surface, place):
    sst, sst_tanh, cur_east, cur_north, rate = [surface[k, place] for k in range(5)]
    east = center[2, 0:1] - cur_east
    north = center[3, 0:1] - cur_north
    factor = rate * jnp.sqrt(1.0 + east * east + north * north)
    return (
        factor * (sst - center[0, 0:1]),
        factor * (sst_tanh - center[1, 0:1]),
        factor * east,
        factor * north,
    )


def tile_state(rows):
    tile = lax.axis_index("tile")
    return lax.rem(tile, 2) == 0, tile * rows


def own_row(north_first, rows, place):
    return jnp.where(north_first, rows - 1 - place, place)


def advance(state, surface, total, weights, staged, turn, valid, updates, count_flux=True):
    places = state.shape[1]
    rows = places - 2 * NSUB
    sign = jnp.where(tile_state(rows)[0], 1.0, -1.0)
    for k, (step, place) in enumerate(updates):
        slot = staged.at[k % staged.shape[0]]
        center, outer, inner = [state.at[step, place + shift] for shift in (0, -1, 1)]
        target = state.at[step + 1, place]
        stage_dynamics(center, outer, inner, sign, turn[place], slot)
        flux = surface_flux(center, surface, place)
        own = NSUB <= place < NSUB + rows
        for f in range(FIELDS):
            mixed = jnp.dot(weights[...], slot[f], preferred_element_type=F32)
            surface_level = mixed[0:1] + (AIR_STEP * SIGNS[f]) * flux[f]
            if own:
                if count_flux:
                    total[place, f] = total[place, f] + flux[f]
                target[f] = mixed
                target[f, 0:1] = surface_level
            else:
                target[f] = valid[place] * mixed
                target[f, 0:1] = valid[place] * surface_level


def pack_kernel(depth, owner, air, sea, first, second, top, sems, top_sems):
    rows = air.shape[2]
    north_first, _ = tile_state(rows)
    copies = []
    for d in range(depth):
        for side, out in enumerate((first, second)):
            row = own_row(north_first, rows, d if side == 0 else rows - 1 - d)
            copies.append(
                pltpu.make_async_copy(air.at[0, :, row], out.at[d], sems.at[2 * d + side])
            )
    tops = [
        pltpu.make_async_copy(sea.at[0, f, 0], top.at[k], top_sems.at[k])
        for k, f in enumerate((0, 2, 3))
    ]
    for copy in tops + copies:
        copy.start()
    for copy in tops:
        copy.wait()

    @pl.when(lax.axis_index("member") != owner[0])
    def _():
        top[...] = jnp.zeros_like(top)

    for copy in copies:
        copy.wait()


def ocean_kernel(scale, owner, coriolis, air, sea, land, air_mixing, sea_mixing, state, weights,
                 base, column, turn, valid, staged, sea_weights, sems, sea_sems):
    rows, lon = air.shape[2], air.shape[4]
    levels = sea.shape[2]
    held, halves = base.shape[2], base.shape[1]
    depth = ceil_to(levels, 16)
    places = rows + 2 * NSUB
    north_first, first_row = tile_state(rows)
    copies = []
    for place in range(rows):
        row = own_row(north_first, rows, place)
        copies.append(
            pltpu.make_async_copy(air.at[0, :, row], state.at[0, NSUB + place], sems.at[place])
        )
    loads = [
        pltpu.make_async_copy(
            sea.at[0, :, :, :, pl.ds(h * LANES, LANES)],
            base.at[:, h, pl.ds(0, levels)],
            sea_sems.at[h],
        )
        for h in range(halves)
    ]
    for copy in loads + copies:
        copy.start()
    weights[...] = mixing_parts(air_mixing[...], 0.5 * DIFFUSE)
    sea_weights[...] = mixing_parts(sea_mixing[...], 0.5)
    total = coriolis.shape[0] - 2 * NSUB
    for place in range(places):
        index = first_row + own_row(north_first, rows, place - NSUB)
        inside = jnp.where((index >= 0) & (index < total), 1.0, 0.0)
        turn[place] = jnp.full((1, lon), coriolis[index + NSUB], F32)
        valid[place] = jnp.full((1, lon), inside, F32)
    owns = lax.axis_index("member") == owner[0]
    factor = jnp.where(owns, 0.5 * scale, 0.0)
    first_column = jnp.broadcast_to(sea_mixing[:, 0:1], (levels, LANES))
    for level in range(levels):
        value = first_column[level : level + 1] + (1.0 if level == 0 else 0.0)
        column[level] = factor * jnp.broadcast_to(value, (rows, LANES))
    if held > levels:
        base[:, :, levels:] = jnp.zeros((FIELDS, halves, held - levels, rows, LANES), F32)
    for load in loads:
        load.wait()

    @pl.when(owns)
    def _():
        flat = base.reshape(FIELDS, halves, held * rows, LANES)

        def body(row, carry):
            own = pl.ds(row, held, stride=rows)
            at_sea = land[pl.ds(row, 1)] == 1
            for f in range(FIELDS):
                cells = jnp.concatenate([flat[f, h, own] for h in range(halves)], axis=1)
                for offset in range(0, held, 16):
                    part = slice(offset, min(offset + 16, held))
                    stage(cells[part], staged.at[f], offset, depth)
                mixed = jnp.dot(sea_weights[...], staged[f], preferred_element_type=F32)
                kept = jnp.where(at_sea, mixed, cells)
                for h in range(halves):
                    flat[f, h, own] = kept[:, h * LANES : (h + 1) * LANES]
            return carry

        lax.fori_loop(0, rows, body, 0)

    for copy in copies:
        copy.wait()


def surface_kernel(top_a, top_b, top_c, top_d, land, transfer, state, surface, first, second):
    rows, lon = land.shape
    levels = state.shape[3]
    last = NSUB + rows - 1
    north_first, _ = tile_state(rows)
    for place in range(rows):
        row = pl.ds(own_row(north_first, rows, place), 1)
        for k, kept in enumerate((0, 2, 3)):
            value = (top_a[k, row] + top_b[k, row]) + (top_c[k, row] + top_d[k, row])
            surface[kept, NSUB + place] = value
        surface[1, NSUB + place] = jnp.tanh(surface[0, NSUB + place])
        surface[4, NSUB + place] = transfer[row] * land[row].astype(F32)
    for side, out in enumerate((first, second)):
        for f in range(FIELDS):
            place = NSUB + 2 if side == 0 else last - 2
            out[f * levels : (f + 1) * levels] = state[0, place, f]
        out[FIELDS * levels :] = jnp.zeros((out.shape[0] - FIELDS * levels, lon), F32)
        for d in range(NSUB - 1):
            place = NSUB + d if side == 0 else last - d
            for k, kept in enumerate((0, 2, 3, 4)):
                at = FIELDS * levels + 4 * d + k
                out[at : at + 1] = surface[kept, place]


def interior_kernel(weights, turn, valid, surface, state_in, state, total, first, second, staged, sems):
    del state_in
    rows = state.shape[1] - 2 * NSUB
    last = NSUB + rows - 1
    copies = [
        pltpu.make_async_copy(state.at[0, NSUB + 3], first, sems.at[0]),
        pltpu.make_async_copy(state.at[0, last - 3], second, sems.at[1]),
    ]
    for copy in copies:
        copy.start()
    total[...] = jnp.zeros_like(total)
    updates = []
    for step in range(NSUB - 1):
        for d in range(step + 1, rows // 2):
            updates += [(step, NSUB + d), (step, last - d)]
    advance(state, surface, total, weights, staged, turn, valid, updates)
    for copy in copies:
        copy.wait()


def take_rows(number, state, valid, row_of):
    places = state.shape[1]
    for side in range(2):
        place = NSUB - number if side == 0 else places - 1 - NSUB + number
        for f in range(FIELDS):
            state[0, place, f] = valid[place] * row_of(side, f)


def chain_step(number, step, state):
    low = NSUB + step + 1 - number
    return [(step, low), (step, state.shape[1] - 1 - low)]


def first_chain_kernel(weights, turn, valid, surface, near, far, state_in, total_in, state, total, staged):
    del state_in, total_in
    for number in (1, 2):
        take_rows(number, state, valid, lambda side, f: (near, far)[side][number - 1, f])
    updates = []
    for step in range(NSUB):
        updates += chain_step(1, step, state)
    advance(state, surface, total, weights, staged, turn, valid, updates)


def flux_chains_kernel(weights, turn, valid, near, far, surface_in, state_in, total_in,
                       surface, state, total, flux, staged):
    del surface_in, state_in, total_in
    places, levels = state.shape[1], state.shape[3]
    rows = places - 2 * NSUB
    arrived = (near, far)
    take_rows(3, state, valid, lambda side, f: arrived[side][f * levels : (f + 1) * levels])
    for side in range(2):
        for d in range(NSUB - 1):
            place = NSUB - 1 - d if side == 0 else places - NSUB + d
            for k, kept in enumerate((0, 2, 3, 4)):
                at = FIELDS * levels + 4 * d + k
                surface[kept, place] = arrived[side][at : at + 1]
            surface[1, place] = jnp.tanh(surface[0, place])
    updates = []
    for step in range(NSUB - 1):
        updates += chain_step(2, step, state) + chain_step(3, step, state)
    advance(state, surface, total, weights, staged, turn, valid, updates)
    for place in range(NSUB, NSUB + rows):
        d = min(place - NSUB, NSUB + rows - 1 - place)
        last = surface_flux(state.at[NSUB - 1, place], surface, place) if d < NSUB - 1 else None
        for f in range(FIELDS):
            value = total[place, f] if last is None else total[place, f] + last[f]
            flux[f, place - NSUB : place - NSUB + 1] = value


def last_chain_kernel(weights, turn, valid, surface, near, far, state_in, state, air_next, staged, sems):
    del state_in
    rows = air_next.shape[2]
    north_first, _ = tile_state(rows)
    arrived = (near, far)

    def send(place):
        row = own_row(north_first, rows, place)
        copy = pltpu.make_async_copy(
            state.at[NSUB, NSUB + place], air_next.at[0, :, row], sems.at[place]
        )
        copy.start()
        return copy

    copies = [send(place) for place in (NSUB - 1, rows - NSUB)]
    take_rows(4, state, valid, lambda side, f: arrived[side][f])
    for d in (2, 1):
        updates = chain_step(NSUB - d, NSUB - 1, state) + chain_step(4, 2 - d, state)
        advance(state, surface, None, weights, staged, turn, valid, updates, False)
        copies += [send(place) for place in (d, rows - 1 - d)]
    updates = chain_step(4, 2, state) + chain_step(4, 3, state)
    advance(state, surface, None, weights, staged, turn, valid, updates, False)
    copies += [send(place) for place in (0, rows - 1)]
    for copy in copies:
        copy.wait()


def sea_kernel(base, column, flux_a, flux_b, flux_c, flux_d, land, after, sea_next, result, mean, sems):
    del after
    rows, levels = land.shape[0], column.shape[0]
    north_first, _ = tile_state(rows)
    at_sea = land[...] == 1
    for f in range(FIELDS):
        for place in range(rows):
            part = slice(place, place + 1)
            value = (flux_a[f, part] + flux_b[f, part]) + (flux_c[f, part] + flux_d[f, part])
            mean[f, pl.ds(own_row(north_first, rows, place), 1)] = value
    copies = []
    for f in range(FIELDS):
        forcing = jnp.where(at_sea, mean[f], 0.0)
        for h in range(base.shape[1]):
            part = forcing[:, h * LANES : (h + 1) * LANES]
            for level in range(levels):
                result[f, h, level] = base[f, h, level] + column[level] * part
            place = sea_next.at[0, f, :, :, pl.ds(h * LANES, LANES)]
            copies.append(pltpu.make_async_copy(result.at[f, h], place, sems.at[f, h]))
            copies[-1].start()
    for copy in copies:
        copy.wait()


def pairings(members, tiles):
    both = []
    for side in range(2):
        pairs = []
        for member in range(members):
            for tile in range(tiles):
                other = tile + 1 if (tile + side) % 2 == 0 else tile - 1
                if 0 <= other < tiles:
                    to = member * tiles + other
                else:
                    to = (member ^ 1) * tiles + tile
                pairs.append((member * tiles + tile, to))
        both.append(pairs)
    return both


def params(**more):
    return pltpu.CompilerParams(vmem_limit_bytes=VMEM_LIMIT, **more)


def cost(microseconds):
    return pl.CostEstimate(flops=0, bytes_accessed=int(microseconds * 3.5e6), transcendentals=0)


def exchange(values, swaps):
    return [lax.ppermute(value, AXES, swap) for value, swap in zip(values, swaps)]


def member_parts(values, members):
    def swapped(block, k):
        return lax.ppermute(block, "member", [(i, i ^ k) for i in range(members)])

    k = 1
    while members > 4 * k:
        values = values + swapped(values, k)
        k *= 2
    parts = [values]
    for other in range(k, members, k):
        parts.append(swapped(values, other))
    return parts


def shards(
    atmos_state, ocean_slots, owner_map, land_mask, transfer_coefficient, air_mixing, sea_mixing
):
    members, tiles = lax.axis_size("member"), lax.axis_size("tile")
    _, _, rows, levels, lon = atmos_state.shape
    sea_levels = ocean_slots.shape[3]
    places = rows + 2 * NSUB
    depth, sea_depth = ceil_to(levels, 16), ceil_to(sea_levels, 16)
    swaps = pairings(members, tiles)
    sea_slots = jnp.swapaxes(ocean_slots, 2, 3)

    row_total = rows * tiles
    row_index = jnp.arange(-NSUB, row_total + NSUB)
    latitude = math.pi * ((row_index.astype(F32) + 0.5) / row_total - 0.5)
    coriolis = (CORIOLIS_MAX / DIFFUSE) * jnp.sin(latitude)

    def rows_of(*count):
        return jax.ShapeDtypeStruct((*count, FIELDS, levels, lon), F32)

    halves, held = lon // LANES, ceil_to(sea_levels, 8)
    state_type = pltpu.VMEM((NSUB + 1, places, FIELDS, levels, lon), F32)
    surface_type = pltpu.VMEM((5, places, 1, lon), F32)
    total_type = pltpu.VMEM((places, FIELDS, 1, lon), F32)
    table_type = pltpu.VMEM((places, 1, lon), F32)
    base_type = pltpu.VMEM((FIELDS, halves, held, rows, LANES), F32)
    topped = jax.ShapeDtypeStruct((ceil_to(FIELDS * levels + 4 * (NSUB - 1), 8), lon), F32)
    staged = pltpu.VMEM((2, FIELDS, 3 * depth, lon), BF16)
    atmos_state = pltpu.with_memory_space_constraint(atmos_state, pltpu.HBM)
    sea_slots = pltpu.with_memory_space_constraint(sea_slots, pltpu.HBM)

    near, far, top = pl.pallas_call(
        functools.partial(pack_kernel, 2),
        name="pack_rows",
        cost_estimate=cost(1.3),
        out_shape=(rows_of(2), rows_of(2), pltpu.VMEM((3, rows, lon), F32)),
        in_specs=[SMEM, ANY, ANY],
        out_specs=(ANY, ANY, VMEM),
        scratch_shapes=[
            pltpu.SemaphoreType.DMA((4,)),
            pltpu.SemaphoreType.DMA((3,)),
        ],
        compiler_params=params(),
    )(owner_map, atmos_state, sea_slots)
    arrived = exchange((near, far), swaps)
    top_parts = member_parts(top, members)

    state, weights, base, column, turn, valid = pl.pallas_call(
        functools.partial(ocean_kernel, SEA_STEP / (NSUB * members)),
        name="sea_mixing",
        cost_estimate=cost(3),
        out_shape=(
            state_type,
            pltpu.VMEM((ceil_to(levels, 8), 3 * depth), BF16),
            base_type,
            pltpu.VMEM((sea_levels, rows, LANES), F32),
            table_type,
            table_type,
        ),
        in_specs=[SMEM, SMEM, ANY, ANY, VMEM, VMEM, VMEM],
        out_specs=(VMEM,) * 6,
        scratch_shapes=[
            pltpu.VMEM((FIELDS, 3 * sea_depth, lon), BF16),
            pltpu.VMEM((held, 3 * sea_depth), BF16),
            pltpu.SemaphoreType.DMA((rows,)),
            pltpu.SemaphoreType.DMA((halves,)),
        ],
        compiler_params=params(),
    )(owner_map, coriolis, atmos_state, sea_slots, land_mask, air_mixing, sea_mixing)
    tables = (weights, turn, valid)

    surface, *third_rows = pl.pallas_call(
        surface_kernel,
        name="surface",
        cost_estimate=cost(0.5),
        out_shape=(surface_type, topped, topped),
        in_specs=[VMEM] * 7,
        out_specs=(VMEM,) * 3,
        compiler_params=params(),
    )(*top_parts, land_mask, transfer_coefficient, state)
    arrived_third = exchange(third_rows, swaps)

    state, total, *fourth_rows = pl.pallas_call(
        interior_kernel,
        name="interior",
        cost_estimate=cost(3),
        out_shape=(state_type, total_type, rows_of(), rows_of()),
        in_specs=[VMEM] * 5,
        out_specs=(VMEM, VMEM, ANY, ANY),
        input_output_aliases={4: 0},
        scratch_shapes=[staged, pltpu.SemaphoreType.DMA((2,))],
        compiler_params=params(),
    )(*tables, surface, state)
    arrived_fourth = exchange(fourth_rows, swaps)

    state, total = pl.pallas_call(
        first_chain_kernel,
        name="first_chain",
        cost_estimate=cost(2),
        out_shape=(state_type, total_type),
        in_specs=[VMEM] * 8,
        out_specs=(VMEM, VMEM),
        input_output_aliases={6: 0, 7: 1},
        scratch_shapes=[staged],
        compiler_params=params(),
    )(*tables, surface, *arrived, state, total)

    surface, state, _, flux = pl.pallas_call(
        flux_chains_kernel,
        name="flux_chains",
        cost_estimate=cost(3),
        out_shape=(surface_type, state_type, total_type, pltpu.VMEM((FIELDS, rows, lon), F32)),
        in_specs=[VMEM] * 8,
        out_specs=(VMEM,) * 4,
        input_output_aliases={5: 0, 6: 1, 7: 2},
        scratch_shapes=[staged],
        compiler_params=params(),
    )(*tables, *arrived_third, surface, state, total)
    flux_parts = member_parts(flux, members)

    _, air_next = pl.pallas_call(
        last_chain_kernel,
        name="last_chain",
        cost_estimate=cost(3.5),
        out_shape=(state_type, pltpu.HBM(atmos_state.shape, F32)),
        in_specs=[VMEM] * 7,
        out_specs=(VMEM, ANY),
        input_output_aliases={6: 0},
        scratch_shapes=[staged, pltpu.SemaphoreType.DMA((rows,))],
        compiler_params=params(),
    )(*tables, surface, *arrived_fourth, state)

    after = pltpu.with_memory_space_constraint(air_next, pltpu.HBM)
    sea_next = pl.pallas_call(
        sea_kernel,
        name="sea_step",
        cost_estimate=cost(1.5),
        out_shape=pltpu.HBM(sea_slots.shape, F32),
        in_specs=[VMEM] * 7 + [ANY],
        out_specs=ANY,
        scratch_shapes=[
            pltpu.VMEM((FIELDS, halves, sea_levels, rows, LANES), F32),
            pltpu.VMEM((FIELDS, rows, lon), F32),
            pltpu.SemaphoreType.DMA((FIELDS, halves)),
        ],
        compiler_params=params(),
    )(base, column, *flux_parts, land_mask, after)
    return (air_next, jnp.swapaxes(sea_next, 2, 3))


def solution(mesh):
    placed = (
        P("member", None, "tile", None, None),
        P("member", None, "tile", None, None),
        P("tile"),
        P("tile", None),
        P("tile", None),
        P(),
        P(),
    )
    return jax.shard_map(
        shards,
        mesh=mesh,
        in_specs=placed,
        out_specs=(P("member", None, "tile", None, None), P("member", None, "tile", None, None)),
        check_vma=False,
    )
```

```python
import functools
import math

import jax
import jax.numpy as jnp
from jax import lax
from jax.experimental import pallas as pl
from jax.experimental.pallas import tpu as pltpu
from jax.sharding import PartitionSpec as P

NSUB = 4
DIFFUSE = 0.2
ADVECT_RATE = 0.15
CORIOLIS_MAX = 0.2
AIR_STEP = 0.05
SEA_STEP = 0.25
SIGNS = (1.0, 1.0, -1.0, -1.0)
FIELDS = 4
LANES = 128
AHEAD = 2
EARLY = 3

F32 = jnp.float32
BF16 = jnp.bfloat16
AXES = ("member", "tile")
VMEM = pl.BlockSpec(memory_space=pltpu.VMEM)
SMEM = pl.BlockSpec(memory_space=pltpu.SMEM)
ANY = pl.BlockSpec(memory_space=pl.ANY)
VMEM_LIMIT = 12 * 2**20


def ceil_to(count, unit):
    return -(-count // unit) * unit


def split_parts(values):
    high = values.astype(BF16).astype(F32)
    return high, (values - high).astype(BF16).astype(F32)


def mixing_parts(mixing, scale):
    levels = mixing.shape[0]
    rows = lax.broadcasted_iota(jnp.int32, mixing.shape, 0)
    columns = lax.broadcasted_iota(jnp.int32, mixing.shape, 1)
    both = scale * mixing + jnp.where(rows == columns, scale, 0.0)
    extra = ceil_to(levels, 8) - levels
    if extra:
        both = jnp.concatenate([both, jnp.zeros((extra, levels), F32)], axis=0)
    high, low = split_parts(both)
    pad = jnp.zeros((both.shape[0], ceil_to(levels, 16) - levels), F32)
    parts = [high, pad, high, pad, low, pad] if pad.shape[1] else [high, high, low]
    return jnp.concatenate(parts, axis=1).astype(BF16)


def stage(cells, staged, offset, depth):
    count, lon = cells.shape
    if count < 16:
        cells = jnp.concatenate([cells, jnp.zeros((16 - count, lon), F32)], axis=0)
    high = cells.astype(BF16)
    low = (cells - high.astype(F32)).astype(BF16)
    staged[offset : offset + 16] = high
    staged[depth + offset : depth + offset + 16] = low
    staged[2 * depth + offset : 2 * depth + offset + 16] = high


def stage_dynamics(center, outer, inner, sign, coriolis, staged):
    levels, lon = center.shape[1:]
    depth = ceil_to(levels, 16)
    rate = 0.5 * ADVECT_RATE / DIFFUSE
    for offset in range(0, levels, 16):
        part = slice(offset, min(offset + 16, levels))
        cells = [center[f, part] for f in range(FIELDS)]
        east_wind = rate * cells[2]
        north_wind = (rate * sign) * cells[3]
        for f in range(FIELDS):
            outer_row, inner_row = outer[f, part], inner[f, part]
            east = pltpu.roll(cells[f], lon - 1, 1)
            west = pltpu.roll(cells[f], 1, 1)
            total = ((east + west) + (outer_row + inner_row)) + cells[f]
            if f < 2:
                total = total - (east_wind * (east - west) + north_wind * (outer_row - inner_row))
            elif f == 2:
                total = total + coriolis * cells[3]
            else:
                total = total - coriolis * cells[2]
            stage(total, staged.at[f], offset, depth)


def surface_flux(center, surface, place):
    sst, sst_tanh, cur_east, cur_north, rate = [surface[k, place] for k in range(5)]
    east = center[2, 0:1] - cur_east
    north = center[3, 0:1] - cur_north
    factor = rate * jnp.sqrt(1.0 + east * east + north * north)
    return (
        factor * (sst - center[0, 0:1]),
        factor * (sst_tanh - center[1, 0:1]),
        factor * east,
        factor * north,
    )


def tile_state(rows):
    tile = lax.axis_index("tile")
    return lax.rem(tile, 2) == 0, tile * rows


def own_row(north_first, rows, place):
    return jnp.where(north_first, rows - 1 - place, place)


def advance(state, surface, total, weights, staged, turn, valid, updates, count_flux=True):
    places = state.shape[1]
    rows = places - 2 * NSUB
    sign = jnp.where(tile_state(rows)[0], 1.0, -1.0)
    for k, (step, place) in enumerate(updates):
        slot = staged.at[k % staged.shape[0]]
        center, outer, inner = [state.at[step, place + shift] for shift in (0, -1, 1)]
        target = state.at[step + 1, place]
        stage_dynamics(center, outer, inner, sign, turn[place], slot)
        flux = surface_flux(center, surface, place)
        own = NSUB <= place < NSUB + rows
        for f in range(FIELDS):
            mixed = jnp.dot(weights[...], slot[f], preferred_element_type=F32)
            surface_level = mixed[0:1] + (AIR_STEP * SIGNS[f]) * flux[f]
            if own:
                if count_flux:
                    total[place, f] = total[place, f] + flux[f]
                target[f] = mixed
                target[f, 0:1] = surface_level
            else:
                target[f] = valid[place] * mixed
                target[f, 0:1] = valid[place] * surface_level


def pack_kernel(air, sea, first, second, top, sems, top_sems):
    rows = air.shape[2]
    north_first, _ = tile_state(rows)
    copies = []
    for d, fields in enumerate((FIELDS, EARLY)):
        for side, out in enumerate((first, second)):
            row = own_row(north_first, rows, d if side == 0 else rows - 1 - d)
            copies.append(
                pltpu.make_async_copy(
                    air.at[0, pl.ds(0, fields), row],
                    out.at[pl.ds(d * FIELDS, fields)],
                    sems.at[2 * d + side],
                )
            )
    tops = [
        pltpu.make_async_copy(sea.at[0, f, 0], top.at[k], top_sems.at[k])
        for k, f in enumerate((0, 2, 3))
    ]
    for copy in copies + tops:
        copy.start()
    for copy in copies + tops:
        copy.wait()


def owner_kernel(owner, top, owned_top):
    owns = lax.axis_index("member") == owner[0]
    owned_top[...] = jnp.where(owns, top[...], 0.0)


def tables_kernel(row_total, scale, owner, air, sea, land_in, transfer, air_mixing_in, sea_mixing_in,
                  state, weights, base, sea_weights, column, turn, valid, rate, land,
                  land_here, transfer_here, air_mixing, sea_mixing, sems, sea_sems, small_sems):
    rows, lon = air.shape[2], air.shape[4]
    levels = sea.shape[2]
    held, halves = base.shape[2], base.shape[1]
    places = rows + 2 * NSUB
    north_first, first_row = tile_state(rows)
    small = [
        pltpu.make_async_copy(source, here, small_sems.at[k])
        for k, (source, here) in enumerate((
            (air_mixing_in, air_mixing), (sea_mixing_in, sea_mixing),
            (land_in, land_here), (transfer, transfer_here),
        ))
    ]
    copies = []
    for place in range(rows):
        row = own_row(north_first, rows, place)
        copies.append(
            pltpu.make_async_copy(air.at[0, :, row], state.at[0, NSUB + place], sems.at[place])
        )
    loads = [
        pltpu.make_async_copy(
            sea.at[0, :, :, :, pl.ds(h * LANES, LANES)],
            base.at[:, h, pl.ds(0, levels)],
            sea_sems.at[h],
        )
        for h in range(halves)
    ]
    for copy in small + copies + loads:
        copy.start()
    if held > levels:
        base[:, :, levels:] = jnp.zeros((FIELDS, halves, held - levels, rows, LANES), F32)
    line = lax.broadcasted_iota(jnp.int32, (places, LANES), 0) - NSUB
    index = first_row + jnp.where(north_first, rows - 1 - line, line)
    latitude = math.pi * ((index.astype(F32) + 0.5) / row_total - 0.5)
    turned = (CORIOLIS_MAX / DIFFUSE) * jnp.sin(latitude)
    inside = jnp.where((index >= 0) & (index < row_total), 1.0, 0.0)
    for place in range(places):
        part = slice(place, place + 1)
        turn[place] = jnp.concatenate([turned[part]] * halves, axis=1)
        valid[place] = jnp.concatenate([inside[part]] * halves, axis=1)
    for copy in small:
        copy.wait()
    weights[...] = mixing_parts(air_mixing[...], 0.5 * DIFFUSE)
    sea_weights[...] = mixing_parts(sea_mixing[...], 0.5)
    factor = jnp.where(lax.axis_index("member") == owner[0], 0.5 * scale, 0.0)
    first_column = jnp.broadcast_to(sea_mixing[:, 0:1], (levels, LANES))
    for level in range(levels):
        value = first_column[level : level + 1] + (1.0 if level == 0 else 0.0)
        column[level] = factor * jnp.broadcast_to(value, (rows, LANES))
    land[...] = land_here[...].astype(F32)
    rate[...] = transfer_here[...] * land[...]
    for copy in copies + loads:
        copy.wait()


def ocean_kernel(owner, land, sea_weights, base_in, after, base, staged):
    del base_in, after
    held, halves, rows = base.shape[2], base.shape[1], base.shape[3]
    depth = staged.shape[1] // 3

    @pl.when(lax.axis_index("member") == owner[0])
    def _():
        flat = base.reshape(FIELDS, halves, held * rows, LANES)

        def body(row, carry):
            own = pl.ds(row, held, stride=rows)
            at_sea = land[pl.ds(row, 1)] == 1.0
            for f in range(FIELDS):
                cells = jnp.concatenate([flat[f, h, own] for h in range(halves)], axis=1)
                for offset in range(0, held, 16):
                    part = slice(offset, min(offset + 16, held))
                    stage(cells[part], staged.at[f], offset, depth)
                mixed = jnp.dot(sea_weights[...], staged[f], preferred_element_type=F32)
                kept = jnp.where(at_sea, mixed, cells)
                for h in range(halves):
                    flat[f, h, own] = kept[:, h * LANES : (h + 1) * LANES]
            return carry

        lax.fori_loop(0, rows, body, 0)


def surface_kernel(top_a, top_b, top_c, top_d, rate, state, surface, first, second):
    levels = state.shape[3]
    rows = rate.shape[0]
    last = NSUB + rows - 1
    north_first, _ = tile_state(rows)
    for place in range(rows):
        row = pl.ds(own_row(north_first, rows, place), 1)
        for k, kept in enumerate((0, 2, 3)):
            value = (top_a[k, row] + top_b[k, row]) + (top_c[k, row] + top_d[k, row])
            surface[kept, NSUB + place] = value
        surface[1, NSUB + place] = jnp.tanh(surface[0, NSUB + place])
        surface[4, NSUB + place] = rate[row]
    for side, out in enumerate((first, second)):
        for f in range(EARLY, FIELDS):
            place = NSUB + 1 if side == 0 else last - 1
            out[(f - EARLY) * levels : (f - EARLY + 1) * levels] = state[0, place, f]
        out[(FIELDS - EARLY) * levels :] = jnp.zeros(
            (out.shape[0] - (FIELDS - EARLY) * levels, out.shape[1]), F32
        )
        for d in range(NSUB - 1):
            place = NSUB + d if side == 0 else last - d
            for k, kept in enumerate((0, 2, 3, 4)):
                at = (FIELDS - EARLY) * levels + 4 * d + k
                out[at : at + 1] = surface[kept, place]


def interior_updates(state, first_d):
    rows = state.shape[1] - 2 * NSUB
    last = NSUB + rows - 1
    updates = []
    for step in range(NSUB - 1):
        for d in range(step + 1, rows // 2):
            updates += [(step, NSUB + d), (step, last - d)]
    return updates[:first_d], updates[first_d:]


def first_interior_kernel(weights, turn, valid, surface, state_in, state, total, first, second, staged, sems):
    del state_in
    last = state.shape[1] - NSUB - 1
    copies = [
        pltpu.make_async_copy(state.at[0, NSUB + 2], first, sems.at[0]),
        pltpu.make_async_copy(state.at[0, last - 2], second, sems.at[1]),
    ]
    for copy in copies:
        copy.start()
    total[...] = jnp.zeros_like(total)
    updates, _ = interior_updates(state, AHEAD)
    advance(state, surface, total, weights, staged, turn, valid, updates)
    for copy in copies:
        copy.wait()


def interior_kernel(weights, turn, valid, surface, near, state_in, total_in, state, total, staged):
    del state_in, total_in
    take_rows(1, state, valid, (lambda f: near[f],))
    _, updates = interior_updates(state, AHEAD)
    advance(state, surface, total, weights, staged, turn, valid, updates)


def take_rows(number, state, valid, row_of, sides=(0, 1)):
    places = state.shape[1]
    for side, row in zip(sides, row_of):
        place = NSUB - number if side == 0 else places - 1 - NSUB + number
        for f in range(FIELDS):
            state[0, place, f] = valid[place] * row(f)


def rows_from(near, far):
    return (lambda f: near[f], lambda f: far[f])


def chain_step(number, step, state):
    low = NSUB + step + 1 - number
    return [(step, low), (step, state.shape[1] - 1 - low)]


def first_chain_kernel(weights, turn, valid, surface, far, state_in, total_in, state, total, staged):
    del state_in, total_in
    take_rows(1, state, valid, (lambda f: far[f],), (1,))
    updates = []
    for step in range(NSUB):
        updates += chain_step(1, step, state)
    advance(state, surface, total, weights, staged, turn, valid, updates)


def second_chain_kernel(weights, turn, valid, near, far, near_rest, far_rest, surface_in, state_in, total_in,
                        surface, state, total, first, second, staged, sems):
    del surface_in, state_in, total_in
    places, levels = state.shape[1], state.shape[3]
    rest = (near_rest, far_rest)
    copies = [
        pltpu.make_async_copy(state.at[0, NSUB + 3], first, sems.at[0]),
        pltpu.make_async_copy(state.at[0, places - NSUB - 4], second, sems.at[1]),
    ]
    for copy in copies:
        copy.start()

    def row_of(side, f):
        if f < EARLY:
            return (near, far)[side][FIELDS + f]
        return rest[side][(f - EARLY) * levels : (f - EARLY + 1) * levels]

    take_rows(2, state, valid, [functools.partial(row_of, side) for side in range(2)])
    for side in range(2):
        for d in range(NSUB - 1):
            place = NSUB - 1 - d if side == 0 else places - NSUB + d
            for k, kept in enumerate((0, 2, 3, 4)):
                at = (FIELDS - EARLY) * levels + 4 * d + k
                surface[kept, place] = rest[side][at : at + 1]
            surface[1, place] = jnp.tanh(surface[0, place])
    updates = []
    for step in range(NSUB - 1):
        updates += chain_step(2, step, state)
    advance(state, surface, total, weights, staged, turn, valid, updates)
    for copy in copies:
        copy.wait()


def third_chain_kernel(weights, turn, valid, surface, near, far, state_in, total_in, state, total, flux, staged):
    del state_in, total_in
    rows = state.shape[1] - 2 * NSUB
    north_first, _ = tile_state(rows)
    take_rows(3, state, valid, rows_from(near, far))
    updates = []
    for step in range(NSUB - 1):
        updates += chain_step(3, step, state)
    advance(state, surface, total, weights, staged, turn, valid, updates)
    for place in range(NSUB, NSUB + rows):
        d = min(place - NSUB, NSUB + rows - 1 - place)
        last = surface_flux(state.at[NSUB - 1, place], surface, place) if d < NSUB - 1 else None
        for f in range(FIELDS):
            value = total[place, f] if last is None else total[place, f] + last[f]
            flux[f, pl.ds(own_row(north_first, rows, place - NSUB), 1)] = value


def finish_kernel(weights, turn, valid, surface, flux_in, state_in, state, flux, staged):
    del state_in
    flux[...] = flux_in[...]
    updates = chain_step(2, NSUB - 1, state) + chain_step(3, NSUB - 1, state)
    advance(state, surface, None, weights, staged, turn, valid, updates, False)


def send_row(state, air_next, place, sem):
    rows = air_next.shape[2]
    row = own_row(tile_state(rows)[0], rows, place)
    copy = pltpu.make_async_copy(state.at[NSUB, NSUB + place], air_next.at[0, :, row], sem)
    copy.start()
    return copy


def last_chain_kernel(weights, turn, valid, surface, near, far, state_in, state, air_next, staged, sems):
    del state_in
    rows = air_next.shape[2]
    copies = [send_row(state, air_next, place, sems.at[place]) for place in range(1, rows - 1)]
    take_rows(4, state, valid, rows_from(near, far))
    updates = []
    for step in range(NSUB):
        updates += chain_step(4, step, state)
    advance(state, surface, None, weights, staged, turn, valid, updates, False)
    for copy in copies:
        copy.wait()


def sea_kernel(base, column, flux_a, flux_b, flux_c, flux_d, state, air_in, sea_next, air_next,
               result, sems, air_sems):
    del air_in
    rows, levels = air_next.shape[2], column.shape[0]
    copies = [
        send_row(state, air_next, place, air_sems.at[k]) for k, place in enumerate((0, rows - 1))
    ]
    for f in range(FIELDS):
        mean = (flux_a[f] + flux_b[f]) + (flux_c[f] + flux_d[f])
        for h in range(base.shape[1]):
            part = mean[:, h * LANES : (h + 1) * LANES]
            for level in range(levels):
                result[f, h, level] = base[f, h, level] + column[level] * part
            place = sea_next.at[0, f, :, :, pl.ds(h * LANES, LANES)]
            copies.append(pltpu.make_async_copy(result.at[f, h], place, sems.at[f, h]))
            copies[-1].start()
    for copy in copies:
        copy.wait()


def pairings(members, tiles):
    both = []
    for side in range(2):
        pairs = []
        for member in range(members):
            for tile in range(tiles):
                other = tile + 1 if (tile + side) % 2 == 0 else tile - 1
                if 0 <= other < tiles:
                    to = member * tiles + other
                else:
                    to = (member ^ 1) * tiles + tile
                pairs.append((member * tiles + tile, to))
        both.append(pairs)
    return both


def params(**more):
    return pltpu.CompilerParams(vmem_limit_bytes=VMEM_LIMIT, **more)


def cost(microseconds):
    return pl.CostEstimate(flops=0, bytes_accessed=int(microseconds * 3.5e6), transcendentals=0)


def exchange(values, swaps):
    return [lax.ppermute(value, AXES, swap) for value, swap in zip(values, swaps)]


def swapped(values, k):
    count = lax.axis_size("member")
    return lax.ppermute(values, "member", [(i, i ^ k) for i in range(count)])


def member_parts(values, then=None):
    k = 1
    while lax.axis_size("member") > 4 * k:
        other = swapped(values, k)
        values = (values if then is None or k > 1 else then()) + other
        k *= 2
    return [values] + [swapped(values, other) for other in range(k, lax.axis_size("member"), k)]


def shards(
    atmos_state, ocean_slots, owner_map, land_mask, transfer_coefficient, air_mixing, sea_mixing
):
    members, tiles = lax.axis_size("member"), lax.axis_size("tile")
    _, _, rows, levels, lon = atmos_state.shape
    sea_levels = ocean_slots.shape[3]
    places = rows + 2 * NSUB
    depth, sea_depth = ceil_to(levels, 16), ceil_to(sea_levels, 16)
    swaps = pairings(members, tiles)
    sea_slots = jnp.swapaxes(ocean_slots, 2, 3)

    def rows_of(*count):
        return jax.ShapeDtypeStruct((*count, FIELDS, levels, lon), F32)

    halves, held = lon // LANES, ceil_to(sea_levels, 8)
    state_type = pltpu.VMEM((NSUB + 1, places, FIELDS, levels, lon), F32)
    surface_type = pltpu.VMEM((5, places, 1, lon), F32)
    total_type = pltpu.VMEM((places, FIELDS, 1, lon), F32)
    table_type = pltpu.VMEM((places, 1, lon), F32)
    base_type = pltpu.VMEM((FIELDS, halves, held, rows, LANES), F32)
    column_type = pltpu.VMEM((sea_levels, rows, LANES), F32)
    sea_weight_type = pltpu.VMEM((held, 3 * sea_depth), BF16)
    cell_type = pltpu.VMEM((rows, lon), F32)
    flux_type = pltpu.VMEM((FIELDS, rows, lon), F32)
    air_type, sea_type = pltpu.HBM(atmos_state.shape, F32), pltpu.HBM(sea_slots.shape, F32)
    topped = pltpu.VMEM((ceil_to((FIELDS - EARLY) * levels + 4 * (NSUB - 1), 8), lon), F32)
    near_type = jax.ShapeDtypeStruct((FIELDS + EARLY, levels, lon), F32)
    staged = pltpu.VMEM((2, FIELDS, 3 * depth, lon), BF16)
    atmos_state, sea_slots, land_cells, transfer, air_square, sea_square = [
        pltpu.with_memory_space_constraint(value, pltpu.HBM)
        for value in (
            atmos_state, sea_slots, land_mask, transfer_coefficient, air_mixing, sea_mixing
        )
    ]

    near, far, top = pl.pallas_call(
        pack_kernel,
        name="pack_rows",
        cost_estimate=cost(1),
        out_shape=(near_type, near_type, pltpu.VMEM((3, rows, lon), F32)),
        in_specs=[ANY, ANY],
        out_specs=(ANY, ANY, VMEM),
        scratch_shapes=[pltpu.SemaphoreType.DMA((4,)), pltpu.SemaphoreType.DMA((3,))],
        compiler_params=params(),
    )(atmos_state, sea_slots)
    top = pl.pallas_call(
        owner_kernel,
        name="owner_surface",
        cost_estimate=cost(0.1),
        out_shape=pltpu.VMEM((3, rows, lon), F32),
        in_specs=[SMEM, VMEM],
        out_specs=VMEM,
        compiler_params=params(),
    )(owner_map, top)
    arrived = exchange((near, far), swaps)
    top_parts = member_parts(top)

    state, weights, base, sea_weights, column, turn, valid, rate, land = pl.pallas_call(
        functools.partial(tables_kernel, rows * tiles, SEA_STEP / (NSUB * members)),
        name="tables",
        cost_estimate=cost(2),
        out_shape=(
            state_type,
            pltpu.VMEM((ceil_to(levels, 8), 3 * depth), BF16),
            base_type,
            sea_weight_type,
            column_type,
            table_type,
            table_type,
            cell_type,
            cell_type,
        ),
        in_specs=[SMEM] + [ANY] * 6,
        out_specs=(VMEM,) * 9,
        scratch_shapes=[
            pltpu.VMEM((rows, lon), jnp.int32),
            pltpu.VMEM((rows, lon), F32),
            pltpu.VMEM(air_mixing.shape, F32),
            pltpu.VMEM(sea_mixing.shape, F32),
            pltpu.SemaphoreType.DMA((rows,)),
            pltpu.SemaphoreType.DMA((halves,)),
            pltpu.SemaphoreType.DMA((4,)),
        ],
        compiler_params=params(),
    )(owner_map, atmos_state, sea_slots, land_cells, transfer, air_square, sea_square)
    tables = (weights, turn, valid)

    surface, *rest_rows = pl.pallas_call(
        surface_kernel,
        name="surface",
        cost_estimate=cost(0.3),
        out_shape=(surface_type, topped, topped),
        in_specs=[VMEM] * 6,
        out_specs=(VMEM,) * 3,
        compiler_params=params(),
    )(*top_parts, rate, state)
    arrived_rest = exchange(rest_rows, swaps)

    state, total, *third_rows = pl.pallas_call(
        first_interior_kernel,
        name="first_interior",
        cost_estimate=cost(0.5),
        out_shape=(state_type, total_type, rows_of(), rows_of()),
        in_specs=[VMEM] * 5,
        out_specs=(VMEM, VMEM, ANY, ANY),
        input_output_aliases={4: 0},
        scratch_shapes=[staged, pltpu.SemaphoreType.DMA((2,))],
        compiler_params=params(),
    )(*tables, surface, state)
    arrived_third = exchange(third_rows, swaps)

    state, total = pl.pallas_call(
        interior_kernel,
        name="interior",
        cost_estimate=cost(2.5),
        out_shape=(state_type, total_type),
        in_specs=[VMEM] * 7,
        out_specs=(VMEM, VMEM),
        input_output_aliases={5: 0, 6: 1},
        scratch_shapes=[staged],
        compiler_params=params(),
    )(*tables, surface, arrived[0], state, total)

    state, total = pl.pallas_call(
        first_chain_kernel,
        name="first_chain",
        cost_estimate=cost(2),
        out_shape=(state_type, total_type),
        in_specs=[VMEM] * 7,
        out_specs=(VMEM, VMEM),
        input_output_aliases={5: 0, 6: 1},
        scratch_shapes=[staged],
        compiler_params=params(),
    )(*tables, surface, arrived[1], state, total)

    base = pl.pallas_call(
        ocean_kernel,
        name="ocean",
        cost_estimate=cost(1.5),
        out_shape=base_type,
        in_specs=[SMEM] + [VMEM] * 4,
        out_specs=VMEM,
        input_output_aliases={3: 0},
        scratch_shapes=[pltpu.VMEM((FIELDS, 3 * sea_depth, lon), BF16)],
        compiler_params=params(),
    )(owner_map, land, sea_weights, base, total)

    surface, state, total, *fourth_rows = pl.pallas_call(
        second_chain_kernel,
        name="second_chain",
        cost_estimate=cost(1.5),
        out_shape=(surface_type, state_type, total_type, rows_of(), rows_of()),
        in_specs=[VMEM] * 10,
        out_specs=(VMEM, VMEM, VMEM, ANY, ANY),
        input_output_aliases={7: 0, 8: 1, 9: 2},
        scratch_shapes=[staged, pltpu.SemaphoreType.DMA((2,))],
        compiler_params=params(),
    )(*tables, *arrived, *arrived_rest, surface, state, total)
    arrived_fourth = exchange(fourth_rows, swaps)

    state, _, flux = pl.pallas_call(
        third_chain_kernel,
        name="third_chain",
        cost_estimate=cost(1.5),
        out_shape=(state_type, total_type, flux_type),
        in_specs=[VMEM] * 8,
        out_specs=(VMEM,) * 3,
        input_output_aliases={6: 0, 7: 1},
        scratch_shapes=[staged],
        compiler_params=params(),
    )(*tables, surface, *arrived_third, state, total)

    def finish():
        nonlocal state
        state, again = pl.pallas_call(
            finish_kernel,
            name="finish",
            cost_estimate=cost(1),
            out_shape=(state_type, flux_type),
            in_specs=[VMEM] * 6,
            out_specs=(VMEM, VMEM),
            input_output_aliases={5: 0},
            scratch_shapes=[staged],
            compiler_params=params(),
        )(*tables, surface, flux, state)
        return again

    flux_parts = member_parts(flux, finish)

    state, air_next = pl.pallas_call(
        last_chain_kernel,
        name="last_chain",
        cost_estimate=cost(2.5),
        out_shape=(state_type, air_type),
        in_specs=[VMEM] * 7,
        out_specs=(VMEM, ANY),
        input_output_aliases={6: 0},
        scratch_shapes=[staged, pltpu.SemaphoreType.DMA((rows,))],
        compiler_params=params(),
    )(*tables, surface, *arrived_fourth, state)

    sea_next, air_next = pl.pallas_call(
        sea_kernel,
        name="sea_step",
        cost_estimate=cost(1.5),
        out_shape=(sea_type, air_type),
        in_specs=[VMEM] * 7 + [ANY],
        out_specs=(ANY, ANY),
        input_output_aliases={7: 1},
        scratch_shapes=[
            pltpu.VMEM((FIELDS, halves, sea_levels, rows, LANES), F32),
            pltpu.SemaphoreType.DMA((FIELDS, halves)),
            pltpu.SemaphoreType.DMA((2,)),
        ],
        compiler_params=params(),
    )(base, column, *flux_parts, state, air_next)
    return (air_next, jnp.swapaxes(sea_next, 2, 3))


def solution(mesh):
    placed = (
        P("member", None, "tile", None, None),
        P("member", None, "tile", None, None),
        P("tile"),
        P("tile", None),
        P("tile", None),
        P(),
        P(),
    )
    return jax.shard_map(
        shards,
        mesh=mesh,
        in_specs=placed,
        out_specs=(P("member", None, "tile", None, None), P("member", None, "tile", None, None)),
        check_vma=False,
    )
```

```python
import functools
import math

import jax
import jax.numpy as jnp
from jax import lax
from jax.experimental import pallas as pl
from jax.experimental.pallas import tpu as pltpu
from jax.sharding import PartitionSpec as P

NSUB = 4
DIFFUSE = 0.2
ADVECT_RATE = 0.15
CORIOLIS_MAX = 0.2
AIR_STEP = 0.05
SEA_STEP = 0.25
SIGNS = (1.0, 1.0, -1.0, -1.0)
FIELDS = 4
LANES = 128
AHEAD = 2
EARLY = 3

F32 = jnp.float32
BF16 = jnp.bfloat16
AXES = ("member", "tile")
VMEM = pl.BlockSpec(memory_space=pltpu.VMEM)
SMEM = pl.BlockSpec(memory_space=pltpu.SMEM)
ANY = pl.BlockSpec(memory_space=pl.ANY)
VMEM_LIMIT = 12 * 2**20


def ceil_to(count, unit):
    return -(-count // unit) * unit


def split_parts(values):
    high = values.astype(BF16).astype(F32)
    return high, (values - high).astype(BF16).astype(F32)


def mixing_parts(mixing, scale):
    levels = mixing.shape[0]
    rows = lax.broadcasted_iota(jnp.int32, mixing.shape, 0)
    columns = lax.broadcasted_iota(jnp.int32, mixing.shape, 1)
    both = scale * mixing + jnp.where(rows == columns, scale, 0.0)
    extra = ceil_to(levels, 8) - levels
    if extra:
        both = jnp.concatenate([both, jnp.zeros((extra, levels), F32)], axis=0)
    high, low = split_parts(both)
    pad = jnp.zeros((both.shape[0], ceil_to(levels, 16) - levels), F32)
    parts = [high, pad, high, pad, low, pad] if pad.shape[1] else [high, high, low]
    return jnp.concatenate(parts, axis=1).astype(BF16)


def stage(cells, staged, offset, depth):
    count, lon = cells.shape
    if count < 16:
        cells = jnp.concatenate([cells, jnp.zeros((16 - count, lon), F32)], axis=0)
    high = cells.astype(BF16)
    low = (cells - high.astype(F32)).astype(BF16)
    staged[offset : offset + 16] = high
    staged[depth + offset : depth + offset + 16] = low
    staged[2 * depth + offset : 2 * depth + offset + 16] = high


def stage_dynamics(center, outer, inner, sign, coriolis, staged):
    levels, lon = center.shape[1:]
    depth = ceil_to(levels, 16)
    rate = 0.5 * ADVECT_RATE / DIFFUSE
    for offset in range(0, levels, 16):
        part = slice(offset, min(offset + 16, levels))
        cells = [center[f, part] for f in range(FIELDS)]
        east_wind = rate * cells[2]
        north_wind = (rate * sign) * cells[3]
        for f in range(FIELDS):
            outer_row, inner_row = outer[f, part], inner[f, part]
            east = pltpu.roll(cells[f], lon - 1, 1)
            west = pltpu.roll(cells[f], 1, 1)
            total = ((east + west) + (outer_row + inner_row)) + cells[f]
            if f < 2:
                total = total - (east_wind * (east - west) + north_wind * (outer_row - inner_row))
            elif f == 2:
                total = total + coriolis * cells[3]
            else:
                total = total - coriolis * cells[2]
            stage(total, staged.at[f], offset, depth)


def surface_flux(center, surface, place):
    sst, sst_tanh, cur_east, cur_north, rate = [surface[k, place] for k in range(5)]
    east = center[2, 0:1] - cur_east
    north = center[3, 0:1] - cur_north
    factor = rate * jnp.sqrt(1.0 + east * east + north * north)
    return (
        factor * (sst - center[0, 0:1]),
        factor * (sst_tanh - center[1, 0:1]),
        factor * east,
        factor * north,
    )


def tile_state(rows):
    tile = lax.axis_index("tile")
    return lax.rem(tile, 2) == 0, tile * rows


def own_row(north_first, rows, place):
    return jnp.where(north_first, rows - 1 - place, place)


def advance(state, surface, total, weights, staged, turn, valid, updates, count_flux=True):
    places = state.shape[1]
    rows = places - 2 * NSUB
    sign = jnp.where(tile_state(rows)[0], 1.0, -1.0)
    for k, (step, place) in enumerate(updates):
        slot = staged.at[k % staged.shape[0]]
        center, outer, inner = [state.at[step, place + shift] for shift in (0, -1, 1)]
        target = state.at[step + 1, place]
        stage_dynamics(center, outer, inner, sign, turn[place], slot)
        flux = surface_flux(center, surface, place)
        own = NSUB <= place < NSUB + rows
        for f in range(FIELDS):
            mixed = jnp.dot(weights[...], slot[f], preferred_element_type=F32)
            surface_level = mixed[0:1] + (AIR_STEP * SIGNS[f]) * flux[f]
            if own:
                if count_flux:
                    total[place, f] = total[place, f] + flux[f]
                target[f] = mixed
                target[f, 0:1] = surface_level
            else:
                target[f] = valid[place] * mixed
                target[f, 0:1] = valid[place] * surface_level


def pack_kernel(air, sea, first, second, top, sems, top_sems):
    rows = air.shape[2]
    north_first, _ = tile_state(rows)
    copies = []
    for d, fields in enumerate((FIELDS, EARLY)):
        for side, out in enumerate((first, second)):
            row = own_row(north_first, rows, d if side == 0 else rows - 1 - d)
            copies.append(
                pltpu.make_async_copy(
                    air.at[0, pl.ds(0, fields), row],
                    out.at[pl.ds(d * FIELDS, fields)],
                    sems.at[2 * d + side],
                )
            )
    tops = [
        pltpu.make_async_copy(sea.at[0, f, 0], top.at[k], top_sems.at[k])
        for k, f in enumerate((0, 2, 3))
    ]
    for copy in copies + tops:
        copy.start()
    for copy in copies + tops:
        copy.wait()


def owner_kernel(owner, top, owned_top):
    owns = lax.axis_index("member") == owner[0]
    owned_top[...] = jnp.where(owns, top[...], 0.0)


def tables_kernel(row_total, scale, owner, air, sea, land_in, transfer, air_mixing_in, sea_mixing_in,
                  state, weights, base, sea_weights, column, turn, valid, rate, land,
                  land_here, transfer_here, air_mixing, sea_mixing, sems, sea_sems, small_sems):
    rows, lon = air.shape[2], air.shape[4]
    levels = sea.shape[2]
    held, halves = base.shape[2], base.shape[1]
    places = rows + 2 * NSUB
    north_first, first_row = tile_state(rows)
    small = [
        pltpu.make_async_copy(source, here, small_sems.at[k])
        for k, (source, here) in enumerate((
            (air_mixing_in, air_mixing), (sea_mixing_in, sea_mixing),
            (land_in, land_here), (transfer, transfer_here),
        ))
    ]
    copies = []
    for place in range(rows):
        row = own_row(north_first, rows, place)
        copies.append(
            pltpu.make_async_copy(air.at[0, :, row], state.at[0, NSUB + place], sems.at[place])
        )
    loads = [
        pltpu.make_async_copy(
            sea.at[0, :, :, :, pl.ds(h * LANES, LANES)],
            base.at[:, h, pl.ds(0, levels)],
            sea_sems.at[h],
        )
        for h in range(halves)
    ]
    for copy in small + copies + loads:
        copy.start()
    if held > levels:
        base[:, :, levels:] = jnp.zeros((FIELDS, halves, held - levels, rows, LANES), F32)
    line = lax.broadcasted_iota(jnp.int32, (places, LANES), 0) - NSUB
    index = first_row + jnp.where(north_first, rows - 1 - line, line)
    latitude = math.pi * ((index.astype(F32) + 0.5) / row_total - 0.5)
    turned = (CORIOLIS_MAX / DIFFUSE) * jnp.sin(latitude)
    inside = jnp.where((index >= 0) & (index < row_total), 1.0, 0.0)
    for place in range(places):
        part = slice(place, place + 1)
        turn[place] = jnp.concatenate([turned[part]] * halves, axis=1)
        valid[place] = jnp.concatenate([inside[part]] * halves, axis=1)
    for copy in small:
        copy.wait()
    weights[...] = mixing_parts(air_mixing[...], 0.5 * DIFFUSE)
    sea_weights[...] = mixing_parts(sea_mixing[...], 0.5)
    factor = jnp.where(lax.axis_index("member") == owner[0], 0.5 * scale, 0.0)
    first_column = jnp.broadcast_to(sea_mixing[:, 0:1], (levels, LANES))
    for level in range(levels):
        value = first_column[level : level + 1] + (1.0 if level == 0 else 0.0)
        column[level] = factor * jnp.broadcast_to(value, (rows, LANES))
    land[...] = land_here[...].astype(F32)
    rate[...] = transfer_here[...] * land[...]
    for copy in copies + loads:
        copy.wait()


def ocean_kernel(owner, land, sea_weights, base_in, state, air_in, base, air_next, sea_next, staged,
                 sems, sea_sems):
    del base_in, air_in
    held, halves, rows = base.shape[2], base.shape[1], base.shape[3]
    depth = staged.shape[1] // 3
    levels = sea_next.shape[2]
    owns = lax.axis_index("member") == owner[0]
    copies = [send_row(state, air_next, place, sems.at[k]) for k, place in enumerate((0, rows - 1))]

    @pl.when(jnp.logical_not(owns))
    def _():
        stores = [
            pltpu.make_async_copy(
                base.at[:, h, pl.ds(0, levels)],
                sea_next.at[0, :, :, :, pl.ds(h * LANES, LANES)],
                sea_sems.at[h],
            )
            for h in range(halves)
        ]
        for store in stores:
            store.start()
        for store in stores:
            store.wait()

    @pl.when(owns)
    def _():
        flat = base.reshape(FIELDS, halves, held * rows, LANES)

        for row in range(rows):
            own = pl.ds(row, held, stride=rows)
            at_sea = land[row : row + 1] == 1.0
            for f in range(FIELDS):
                slot = staged.at[(row * FIELDS + f) % staged.shape[0]]
                cells = jnp.concatenate([flat[f, h, own] for h in range(halves)], axis=1)
                for offset in range(0, held, 16):
                    part = slice(offset, min(offset + 16, held))
                    stage(cells[part], slot, offset, depth)
                mixed = jnp.dot(sea_weights[...], slot[...], preferred_element_type=F32)
                kept = jnp.where(at_sea, mixed, cells)
                for h in range(halves):
                    flat[f, h, own] = kept[:, h * LANES : (h + 1) * LANES]

    for copy in copies:
        copy.wait()


def surface_kernel(top_a, top_b, top_c, top_d, rate, state, surface, first, second):
    levels = state.shape[3]
    rows = rate.shape[0]
    last = NSUB + rows - 1
    north_first, _ = tile_state(rows)
    for place in range(rows):
        row = pl.ds(own_row(north_first, rows, place), 1)
        for k, kept in enumerate((0, 2, 3)):
            value = (top_a[k, row] + top_b[k, row]) + (top_c[k, row] + top_d[k, row])
            surface[kept, NSUB + place] = value
        surface[1, NSUB + place] = jnp.tanh(surface[0, NSUB + place])
        surface[4, NSUB + place] = rate[row]
    for side, out in enumerate((first, second)):
        for f in range(EARLY, FIELDS):
            place = NSUB + 1 if side == 0 else last - 1
            out[(f - EARLY) * levels : (f - EARLY + 1) * levels] = state[0, place, f]
        out[(FIELDS - EARLY) * levels :] = jnp.zeros(
            (out.shape[0] - (FIELDS - EARLY) * levels, out.shape[1]), F32
        )
        for d in range(NSUB - 1):
            place = NSUB + d if side == 0 else last - d
            for k, kept in enumerate((0, 2, 3, 4)):
                at = (FIELDS - EARLY) * levels + 4 * d + k
                out[at : at + 1] = surface[kept, place]


def interior_updates(state, first_d):
    rows = state.shape[1] - 2 * NSUB
    last = NSUB + rows - 1
    updates = []
    for step in range(NSUB - 1):
        for d in range(step + 1, rows // 2):
            updates += [(step, NSUB + d), (step, last - d)]
    return updates[:first_d], updates[first_d:]


def first_interior_kernel(weights, turn, valid, surface, state_in, state, total, first, second, staged, sems):
    del state_in
    last = state.shape[1] - NSUB - 1
    copies = [
        pltpu.make_async_copy(state.at[0, NSUB + 2], first, sems.at[0]),
        pltpu.make_async_copy(state.at[0, last - 2], second, sems.at[1]),
    ]
    for copy in copies:
        copy.start()
    total[...] = jnp.zeros_like(total)
    updates, _ = interior_updates(state, AHEAD)
    advance(state, surface, total, weights, staged, turn, valid, updates)
    for copy in copies:
        copy.wait()


def interior_kernel(weights, turn, valid, surface, near, state_in, total_in, state, total, staged):
    del state_in, total_in
    take_rows(1, state, valid, (lambda f: near[f],))
    _, updates = interior_updates(state, AHEAD)
    advance(state, surface, total, weights, staged, turn, valid, updates)


def take_rows(number, state, valid, row_of, sides=(0, 1)):
    places = state.shape[1]
    for side, row in zip(sides, row_of):
        place = NSUB - number if side == 0 else places - 1 - NSUB + number
        for f in range(FIELDS):
            state[0, place, f] = valid[place] * row(f)


def rows_from(near, far):
    return (lambda f: near[f], lambda f: far[f])


def chain_step(number, step, state):
    low = NSUB + step + 1 - number
    return [(step, low), (step, state.shape[1] - 1 - low)]


def first_chain_kernel(weights, turn, valid, surface, far, state_in, total_in, state, total, staged):
    del state_in, total_in
    take_rows(1, state, valid, (lambda f: far[f],), (1,))
    updates = []
    for step in range(NSUB):
        updates += chain_step(1, step, state)
    advance(state, surface, total, weights, staged, turn, valid, updates)


def second_chain_kernel(weights, turn, valid, near, far, near_rest, far_rest, surface_in, state_in, total_in,
                        surface, state, total, first, second, staged, sems):
    del surface_in, state_in, total_in
    places, levels = state.shape[1], state.shape[3]
    rest = (near_rest, far_rest)
    copies = [
        pltpu.make_async_copy(state.at[0, NSUB + 3], first, sems.at[0]),
        pltpu.make_async_copy(state.at[0, places - NSUB - 4], second, sems.at[1]),
    ]
    for copy in copies:
        copy.start()

    def row_of(side, f):
        if f < EARLY:
            return (near, far)[side][FIELDS + f]
        return rest[side][(f - EARLY) * levels : (f - EARLY + 1) * levels]

    take_rows(2, state, valid, [functools.partial(row_of, side) for side in range(2)])
    for side in range(2):
        for d in range(NSUB - 1):
            place = NSUB - 1 - d if side == 0 else places - NSUB + d
            for k, kept in enumerate((0, 2, 3, 4)):
                at = (FIELDS - EARLY) * levels + 4 * d + k
                surface[kept, place] = rest[side][at : at + 1]
            surface[1, place] = jnp.tanh(surface[0, place])
    updates = []
    for step in range(NSUB - 1):
        updates += chain_step(2, step, state)
    advance(state, surface, total, weights, staged, turn, valid, updates)
    for copy in copies:
        copy.wait()


def third_chain_kernel(weights, turn, valid, surface, near, far, state_in, total_in, state, total, flux, staged):
    del state_in, total_in
    rows = state.shape[1] - 2 * NSUB
    north_first, _ = tile_state(rows)
    take_rows(3, state, valid, rows_from(near, far))
    updates = []
    for step in range(NSUB - 1):
        updates += chain_step(3, step, state)
    advance(state, surface, total, weights, staged, turn, valid, updates)
    for place in range(NSUB, NSUB + rows):
        d = min(place - NSUB, NSUB + rows - 1 - place)
        last = surface_flux(state.at[NSUB - 1, place], surface, place) if d < NSUB - 1 else None
        for f in range(FIELDS):
            value = total[place, f] if last is None else total[place, f] + last[f]
            flux[f, pl.ds(own_row(north_first, rows, place - NSUB), 1)] = value


def finish_kernel(weights, turn, valid, surface, flux_in, state_in, state, flux, staged):
    del state_in
    flux[...] = flux_in[...]
    updates = chain_step(2, NSUB - 1, state) + chain_step(3, NSUB - 1, state)
    advance(state, surface, None, weights, staged, turn, valid, updates, False)


def send_row(state, air_next, place, sem):
    rows = air_next.shape[2]
    row = own_row(tile_state(rows)[0], rows, place)
    copy = pltpu.make_async_copy(state.at[NSUB, NSUB + place], air_next.at[0, :, row], sem)
    copy.start()
    return copy


def last_chain_kernel(weights, turn, valid, surface, near, far, state_in, state, air_next, staged, sems):
    del state_in
    rows = air_next.shape[2]
    copies = [send_row(state, air_next, place, sems.at[place]) for place in range(1, rows - 1)]
    take_rows(4, state, valid, rows_from(near, far))
    updates = []
    for step in range(NSUB):
        updates += chain_step(4, step, state)
    advance(state, surface, None, weights, staged, turn, valid, updates, False)
    for copy in copies:
        copy.wait()


def sea_kernel(owner, base, column, flux_a, flux_b, flux_c, flux_d, sea_in, sea_next, result, sems):
    del sea_in
    levels = column.shape[0]

    @pl.when(lax.axis_index("member") == owner[0])
    def _():
        copies = []
        for f in range(FIELDS):
            mean = (flux_a[f] + flux_b[f]) + (flux_c[f] + flux_d[f])
            for h in range(base.shape[1]):
                part = mean[:, h * LANES : (h + 1) * LANES]
                for level in range(levels):
                    result[f, h, level] = base[f, h, level] + column[level] * part
                place = sea_next.at[0, f, :, :, pl.ds(h * LANES, LANES)]
                copies.append(pltpu.make_async_copy(result.at[f, h], place, sems.at[f, h]))
                copies[-1].start()
        for copy in copies:
            copy.wait()


def pairings(members, tiles):
    both = []
    for side in range(2):
        pairs = []
        for member in range(members):
            for tile in range(tiles):
                other = tile + 1 if (tile + side) % 2 == 0 else tile - 1
                if 0 <= other < tiles:
                    to = member * tiles + other
                else:
                    to = (member ^ 1) * tiles + tile
                pairs.append((member * tiles + tile, to))
        both.append(pairs)
    return both


def params(**more):
    return pltpu.CompilerParams(vmem_limit_bytes=VMEM_LIMIT, **more)


def cost(microseconds):
    return pl.CostEstimate(flops=0, bytes_accessed=int(microseconds * 3.5e6), transcendentals=0)


def exchange(values, swaps):
    return [lax.ppermute(value, AXES, swap) for value, swap in zip(values, swaps)]


def swapped(values, k):
    count = lax.axis_size("member")
    return lax.ppermute(values, "member", [(i, i ^ k) for i in range(count)])


def member_parts(values, then=None):
    k = 1
    while lax.axis_size("member") > 4 * k:
        other = swapped(values, k)
        values = (values if then is None or k > 1 else then()) + other
        k *= 2
    others = range(lax.axis_size("member") - k, 0, -k)
    return [values] + [swapped(values, other) for other in others]


def shards(
    atmos_state, ocean_slots, owner_map, land_mask, transfer_coefficient, air_mixing, sea_mixing
):
    members, tiles = lax.axis_size("member"), lax.axis_size("tile")
    _, _, rows, levels, lon = atmos_state.shape
    sea_levels = ocean_slots.shape[3]
    places = rows + 2 * NSUB
    depth, sea_depth = ceil_to(levels, 16), ceil_to(sea_levels, 16)
    swaps = pairings(members, tiles)
    sea_slots = jnp.swapaxes(ocean_slots, 2, 3)

    def rows_of(*count):
        return jax.ShapeDtypeStruct((*count, FIELDS, levels, lon), F32)

    halves, held = lon // LANES, ceil_to(sea_levels, 8)
    state_type = pltpu.VMEM((NSUB + 1, places, FIELDS, levels, lon), F32)
    surface_type = pltpu.VMEM((5, places, 1, lon), F32)
    total_type = pltpu.VMEM((places, FIELDS, 1, lon), F32)
    table_type = pltpu.VMEM((places, 1, lon), F32)
    base_type = pltpu.VMEM((FIELDS, halves, held, rows, LANES), F32)
    column_type = pltpu.VMEM((sea_levels, rows, LANES), F32)
    sea_weight_type = pltpu.VMEM((held, 3 * sea_depth), BF16)
    cell_type = pltpu.VMEM((rows, lon), F32)
    flux_type = pltpu.VMEM((FIELDS, rows, lon), F32)
    air_type, sea_type = pltpu.HBM(atmos_state.shape, F32), pltpu.HBM(sea_slots.shape, F32)
    topped = pltpu.VMEM((ceil_to((FIELDS - EARLY) * levels + 4 * (NSUB - 1), 8), lon), F32)
    near_type = jax.ShapeDtypeStruct((FIELDS + EARLY, levels, lon), F32)
    staged = pltpu.VMEM((2, FIELDS, 3 * depth, lon), BF16)
    atmos_state, sea_slots, land_cells, transfer, air_square, sea_square = [
        pltpu.with_memory_space_constraint(value, pltpu.HBM)
        for value in (
            atmos_state, sea_slots, land_mask, transfer_coefficient, air_mixing, sea_mixing
        )
    ]

    near, far, top = pl.pallas_call(
        pack_kernel,
        name="pack_rows",
        cost_estimate=cost(1),
        out_shape=(near_type, near_type, pltpu.VMEM((3, rows, lon), F32)),
        in_specs=[ANY, ANY],
        out_specs=(ANY, ANY, VMEM),
        scratch_shapes=[pltpu.SemaphoreType.DMA((4,)), pltpu.SemaphoreType.DMA((3,))],
        compiler_params=params(),
    )(atmos_state, sea_slots)
    top = pl.pallas_call(
        owner_kernel,
        name="owner_surface",
        cost_estimate=cost(0.1),
        out_shape=pltpu.VMEM((3, rows, lon), F32),
        in_specs=[SMEM, VMEM],
        out_specs=VMEM,
        compiler_params=params(),
    )(owner_map, top)
    arrived = exchange((near, far), swaps)
    top_parts = member_parts(top)

    state, weights, base, sea_weights, column, turn, valid, rate, land = pl.pallas_call(
        functools.partial(tables_kernel, rows * tiles, SEA_STEP / (NSUB * members)),
        name="tables",
        cost_estimate=cost(2),
        out_shape=(
            state_type,
            pltpu.VMEM((ceil_to(levels, 8), 3 * depth), BF16),
            base_type,
            sea_weight_type,
            column_type,
            table_type,
            table_type,
            cell_type,
            cell_type,
        ),
        in_specs=[SMEM] + [ANY] * 6,
        out_specs=(VMEM,) * 9,
        scratch_shapes=[
            pltpu.VMEM((rows, lon), jnp.int32),
            pltpu.VMEM((rows, lon), F32),
            pltpu.VMEM(air_mixing.shape, F32),
            pltpu.VMEM(sea_mixing.shape, F32),
            pltpu.SemaphoreType.DMA((rows,)),
            pltpu.SemaphoreType.DMA((halves,)),
            pltpu.SemaphoreType.DMA((4,)),
        ],
        compiler_params=params(),
    )(owner_map, atmos_state, sea_slots, land_cells, transfer, air_square, sea_square)
    tables = (weights, turn, valid)

    surface, *rest_rows = pl.pallas_call(
        surface_kernel,
        name="surface",
        cost_estimate=cost(0.3),
        out_shape=(surface_type, topped, topped),
        in_specs=[VMEM] * 6,
        out_specs=(VMEM,) * 3,
        compiler_params=params(),
    )(*top_parts, rate, state)
    arrived_rest = exchange(rest_rows, swaps)

    state, total, *third_rows = pl.pallas_call(
        first_interior_kernel,
        name="first_interior",
        cost_estimate=cost(0.5),
        out_shape=(state_type, total_type, rows_of(), rows_of()),
        in_specs=[VMEM] * 5,
        out_specs=(VMEM, VMEM, ANY, ANY),
        input_output_aliases={4: 0},
        scratch_shapes=[staged, pltpu.SemaphoreType.DMA((2,))],
        compiler_params=params(),
    )(*tables, surface, state)
    arrived_third = exchange(third_rows, swaps)

    state, total = pl.pallas_call(
        interior_kernel,
        name="interior",
        cost_estimate=cost(2.5),
        out_shape=(state_type, total_type),
        in_specs=[VMEM] * 7,
        out_specs=(VMEM, VMEM),
        input_output_aliases={5: 0, 6: 1},
        scratch_shapes=[staged],
        compiler_params=params(),
    )(*tables, surface, arrived[0], state, total)

    state, total = pl.pallas_call(
        first_chain_kernel,
        name="first_chain",
        cost_estimate=cost(2),
        out_shape=(state_type, total_type),
        in_specs=[VMEM] * 7,
        out_specs=(VMEM, VMEM),
        input_output_aliases={5: 0, 6: 1},
        scratch_shapes=[staged],
        compiler_params=params(),
    )(*tables, surface, arrived[1], state, total)

    surface, state, total, *fourth_rows = pl.pallas_call(
        second_chain_kernel,
        name="second_chain",
        cost_estimate=cost(1.5),
        out_shape=(surface_type, state_type, total_type, rows_of(), rows_of()),
        in_specs=[VMEM] * 10,
        out_specs=(VMEM, VMEM, VMEM, ANY, ANY),
        input_output_aliases={7: 0, 8: 1, 9: 2},
        scratch_shapes=[staged, pltpu.SemaphoreType.DMA((2,))],
        compiler_params=params(),
    )(*tables, *arrived, *arrived_rest, surface, state, total)
    arrived_fourth = exchange(fourth_rows, swaps)

    state, _, flux = pl.pallas_call(
        third_chain_kernel,
        name="third_chain",
        cost_estimate=cost(1.5),
        out_shape=(state_type, total_type, flux_type),
        in_specs=[VMEM] * 8,
        out_specs=(VMEM,) * 3,
        input_output_aliases={6: 0, 7: 1},
        scratch_shapes=[staged],
        compiler_params=params(),
    )(*tables, surface, *arrived_third, state, total)

    def finish():
        nonlocal state
        state, again = pl.pallas_call(
            finish_kernel,
            name="finish",
            cost_estimate=cost(1),
            out_shape=(state_type, flux_type),
            in_specs=[VMEM] * 6,
            out_specs=(VMEM, VMEM),
            input_output_aliases={5: 0},
            scratch_shapes=[staged],
            compiler_params=params(),
        )(*tables, surface, flux, state)
        return again

    flux_parts = member_parts(flux, finish)

    state, air_next = pl.pallas_call(
        last_chain_kernel,
        name="last_chain",
        cost_estimate=cost(2.5),
        out_shape=(state_type, air_type),
        in_specs=[VMEM] * 7,
        out_specs=(VMEM, ANY),
        input_output_aliases={6: 0},
        scratch_shapes=[staged, pltpu.SemaphoreType.DMA((rows,))],
        compiler_params=params(),
    )(*tables, surface, *arrived_fourth, state)

    base, air_next, sea_next = pl.pallas_call(
        ocean_kernel,
        name="ocean",
        cost_estimate=cost(1.5),
        out_shape=(base_type, air_type, sea_type),
        in_specs=[SMEM] + [VMEM] * 4 + [ANY],
        out_specs=(VMEM, ANY, ANY),
        input_output_aliases={3: 0, 5: 1},
        scratch_shapes=[
            pltpu.VMEM((2 * FIELDS, 3 * sea_depth, lon), BF16),
            pltpu.SemaphoreType.DMA((2,)),
            pltpu.SemaphoreType.DMA((halves,)),
        ],
        compiler_params=params(),
    )(owner_map, land, sea_weights, base, state, air_next)

    sea_next = pl.pallas_call(
        sea_kernel,
        name="sea_step",
        cost_estimate=cost(1.5),
        out_shape=sea_type,
        in_specs=[SMEM] + [VMEM] * 6 + [ANY],
        out_specs=ANY,
        input_output_aliases={7: 0},
        scratch_shapes=[
            pltpu.VMEM((FIELDS, halves, sea_levels, rows, LANES), F32),
            pltpu.SemaphoreType.DMA((FIELDS, halves)),
        ],
        compiler_params=params(),
    )(owner_map, base, column, *flux_parts, sea_next)
    return (air_next, jnp.swapaxes(sea_next, 2, 3))


def solution(mesh):
    placed = (
        P("member", None, "tile", None, None),
        P("member", None, "tile", None, None),
        P("tile"),
        P("tile", None),
        P("tile", None),
        P(),
        P(),
    )
    return jax.shard_map(
        shards,
        mesh=mesh,
        in_specs=placed,
        out_specs=(P("member", None, "tile", None, None), P("member", None, "tile", None, None)),
        check_vma=False,
    )
```

```python
import functools
import math

import jax
import jax.numpy as jnp
from jax import lax
from jax.experimental import pallas as pl
from jax.experimental.pallas import tpu as pltpu
from jax.sharding import PartitionSpec as P

NSUB = 4
DIFFUSE = 0.2
ADVECT_RATE = 0.15
CORIOLIS_MAX = 0.2
AIR_STEP = 0.05
SEA_STEP = 0.25
SIGNS = (1.0, 1.0, -1.0, -1.0)
FIELDS = 4
LANES = 128
AHEAD = 0
EARLY = (3, 3)

F32 = jnp.float32
BF16 = jnp.bfloat16
AXES = ("member", "tile")
VMEM = pl.BlockSpec(memory_space=pltpu.VMEM)
SMEM = pl.BlockSpec(memory_space=pltpu.SMEM)
ANY = pl.BlockSpec(memory_space=pl.ANY)
VMEM_LIMIT = 12 * 2**20


def ceil_to(count, unit):
    return -(-count // unit) * unit


def split_parts(values):
    high = values.astype(BF16).astype(F32)
    return high, (values - high).astype(BF16).astype(F32)


def mixing_parts(mixing, scale):
    levels = mixing.shape[0]
    rows = lax.broadcasted_iota(jnp.int32, mixing.shape, 0)
    columns = lax.broadcasted_iota(jnp.int32, mixing.shape, 1)
    both = scale * mixing + jnp.where(rows == columns, scale, 0.0)
    extra = ceil_to(levels, 8) - levels
    if extra:
        both = jnp.concatenate([both, jnp.zeros((extra, levels), F32)], axis=0)
    high, low = split_parts(both)
    pad = jnp.zeros((both.shape[0], ceil_to(levels, 16) - levels), F32)
    parts = [high, pad, high, pad, low, pad] if pad.shape[1] else [high, high, low]
    return jnp.concatenate(parts, axis=1).astype(BF16)


def stage(cells, staged, offset, depth):
    count, lon = cells.shape
    if count < 16:
        cells = jnp.concatenate([cells, jnp.zeros((16 - count, lon), F32)], axis=0)
    high = cells.astype(BF16)
    low = (cells - high.astype(F32)).astype(BF16)
    staged[offset : offset + 16] = high
    staged[depth + offset : depth + offset + 16] = low
    staged[2 * depth + offset : 2 * depth + offset + 16] = high


def stage_dynamics(center, outer, inner, sign, coriolis, staged):
    levels, lon = center.shape[1:]
    depth = ceil_to(levels, 16)
    rate = 0.5 * ADVECT_RATE / DIFFUSE
    for offset in range(0, levels, 16):
        part = slice(offset, min(offset + 16, levels))
        cells = [center[f, part] for f in range(FIELDS)]
        east_wind = rate * cells[2]
        north_wind = (rate * sign) * cells[3]
        for f in range(FIELDS):
            outer_row, inner_row = outer[f, part], inner[f, part]
            east = pltpu.roll(cells[f], lon - 1, 1)
            west = pltpu.roll(cells[f], 1, 1)
            total = ((east + west) + (outer_row + inner_row)) + cells[f]
            if f < 2:
                total = total - (east_wind * (east - west) + north_wind * (outer_row - inner_row))
            elif f == 2:
                total = total + coriolis * cells[3]
            else:
                total = total - coriolis * cells[2]
            stage(total, staged.at[f], offset, depth)


def surface_flux(center, surface, place):
    sst, sst_tanh, cur_east, cur_north, rate = [surface[k, place] for k in range(5)]
    east = center[2, 0:1] - cur_east
    north = center[3, 0:1] - cur_north
    factor = rate * jnp.sqrt(1.0 + east * east + north * north)
    return (
        factor * (sst - center[0, 0:1]),
        factor * (sst_tanh - center[1, 0:1]),
        factor * east,
        factor * north,
    )


def tile_state(rows):
    tile = lax.axis_index("tile")
    return lax.rem(tile, 2) == 0, tile * rows


def own_row(north_first, rows, place):
    return jnp.where(north_first, rows - 1 - place, place)


def advance(state, surface, total, weights, staged, turn, valid, updates, count_flux=True):
    places = state.shape[1]
    rows = places - 2 * NSUB
    sign = jnp.where(tile_state(rows)[0], 1.0, -1.0)
    for k, (step, place) in enumerate(updates):
        slot = staged.at[k % staged.shape[0]]
        center, outer, inner = [state.at[step, place + shift] for shift in (0, -1, 1)]
        target = state.at[step + 1, place]
        stage_dynamics(center, outer, inner, sign, turn[place], slot)
        flux = surface_flux(center, surface, place)
        own = NSUB <= place < NSUB + rows
        kind = 0 if own else 1 if place < NSUB else 2
        for f in range(FIELDS):
            if own and count_flux:
                total[place, f] = total[place, f] + flux[f]
            mixed = jnp.dot(weights[kind], slot[f], preferred_element_type=F32)
            added = (AIR_STEP * SIGNS[f]) * flux[f]
            target[f] = mixed
            target[f, 0:1] = mixed[0:1] + (added if own else valid[place] * added)


def pack_kernel(air, sea, first, second, top, sems, top_sems):
    rows = air.shape[2]
    north_first, _ = tile_state(rows)
    copies = []
    for d in range(2):
        for side, out in enumerate((first, second)):
            fields = FIELDS if d == 0 else EARLY[side]
            row = own_row(north_first, rows, d if side == 0 else rows - 1 - d)
            copies.append(
                pltpu.make_async_copy(
                    air.at[0, pl.ds(0, fields), row],
                    out.at[pl.ds(d * FIELDS, fields)],
                    sems.at[2 * d + side],
                )
            )
    tops = [
        pltpu.make_async_copy(sea.at[0, f, 0], top.at[k], top_sems.at[k])
        for k, f in enumerate((0, 2, 3))
    ]
    for copy in copies + tops:
        copy.start()
    for copy in copies + tops:
        copy.wait()


def owner_kernel(owner, top, owned_top):
    owns = lax.axis_index("member") == owner[0]
    owned_top[...] = jnp.where(owns, top[...], 0.0)


def sea_tables_kernel(scale, owner, sea, land_in, sea_mixing_in, top_in, base, sea_weights, column, land, top,
                      land_here, sea_mixing, sems, small_sems):
    rows, levels = land.shape[0], sea.shape[2]
    held, halves = base.shape[2], base.shape[1]
    small = [
        pltpu.make_async_copy(source, here, small_sems.at[k])
        for k, (source, here) in enumerate(((sea_mixing_in, sea_mixing), (land_in, land_here)))
    ]
    loads = [
        pltpu.make_async_copy(
            sea.at[0, :, :, :, pl.ds(h * LANES, LANES)],
            base.at[:, h, pl.ds(0, levels)],
            sems.at[h],
        )
        for h in range(halves)
    ]
    for copy in small + loads:
        copy.start()
    top[...] = top_in[...]
    if held > levels:
        base[:, :, levels:] = jnp.zeros((FIELDS, halves, held - levels, rows, LANES), F32)
    for copy in small:
        copy.wait()
    land[...] = land_here[...].astype(F32)
    sea_weights[...] = mixing_parts(sea_mixing[...], 0.5)
    factor = jnp.where(lax.axis_index("member") == owner[0], 0.5 * scale, 0.0)
    first_column = jnp.broadcast_to(sea_mixing[:, 0:1], (levels, LANES))
    for level in range(levels):
        value = first_column[level : level + 1] + (1.0 if level == 0 else 0.0)
        column[level] = factor * jnp.broadcast_to(value, (rows, LANES))
    for copy in loads:
        copy.wait()


def tables_kernel(row_total, air, transfer, air_mixing_in, land, after, state, weights, turn, valid, rate,
                  transfer_here, air_mixing, sems, small_sems):
    del after
    rows, lon = air.shape[2], air.shape[4]
    halves, places = lon // LANES, rows + 2 * NSUB
    north_first, first_row = tile_state(rows)
    small = [
        pltpu.make_async_copy(source, here, small_sems.at[k])
        for k, (source, here) in enumerate(((air_mixing_in, air_mixing), (transfer, transfer_here)))
    ]
    copies = []
    for place in range(rows):
        row = own_row(north_first, rows, place)
        copies.append(
            pltpu.make_async_copy(air.at[0, :, row], state.at[0, NSUB + place], sems.at[place])
        )
    for copy in small + copies:
        copy.start()
    line = lax.broadcasted_iota(jnp.int32, (places, LANES), 0) - NSUB
    index = first_row + jnp.where(north_first, rows - 1 - line, line)
    latitude = math.pi * ((index.astype(F32) + 0.5) / row_total - 0.5)
    turned = (CORIOLIS_MAX / DIFFUSE) * jnp.sin(latitude)
    inside = jnp.where((index >= 0) & (index < row_total), 1.0, 0.0)
    for place in range(places):
        part = slice(place, place + 1)
        turn[place] = jnp.concatenate([turned[part]] * halves, axis=1)
        valid[place] = jnp.concatenate([inside[part]] * halves, axis=1)
    for copy in small:
        copy.wait()
    parts = mixing_parts(air_mixing[...], 0.5 * DIFFUSE)
    weights[0] = parts
    for side, place in enumerate((NSUB - 1, NSUB + rows)):
        exists = valid[place, 0:1, 0:1].astype(BF16)
        weights[1 + side] = parts * exists
    rate[...] = transfer_here[...] * land[...]
    for copy in copies:
        copy.wait()


def ocean_kernel(owner, land, sea_weights, base_in, base, sea_next, staged, sea_sems):
    del base_in
    held, halves, rows = base.shape[2], base.shape[1], base.shape[3]
    depth = staged.shape[1] // 3
    levels = sea_next.shape[2]
    owns = lax.axis_index("member") == owner[0]

    @pl.when(jnp.logical_not(owns))
    def _():
        stores = [
            pltpu.make_async_copy(
                base.at[:, h, pl.ds(0, levels)],
                sea_next.at[0, :, :, :, pl.ds(h * LANES, LANES)],
                sea_sems.at[h],
            )
            for h in range(halves)
        ]
        for store in stores:
            store.start()
        for store in stores:
            store.wait()

    @pl.when(owns)
    def _():
        flat = base.reshape(FIELDS, halves, held * rows, LANES)

        for row in range(rows):
            own = pl.ds(row, held, stride=rows)
            at_sea = land[row : row + 1] == 1.0
            for f in range(FIELDS):
                slot = staged.at[(row * FIELDS + f) % staged.shape[0]]
                cells = jnp.concatenate([flat[f, h, own] for h in range(halves)], axis=1)
                for offset in range(0, held, 16):
                    part = slice(offset, min(offset + 16, held))
                    stage(cells[part], slot, offset, depth)
                mixed = jnp.dot(sea_weights[...], slot[...], preferred_element_type=F32)
                kept = jnp.where(at_sea, mixed, cells)
                for h in range(halves):
                    flat[f, h, own] = kept[:, h * LANES : (h + 1) * LANES]


def surface_kernel(top_a, top_b, top_c, top_d, rate, state, surface, first, second):
    levels = state.shape[3]
    rows = rate.shape[0]
    last = NSUB + rows - 1
    north_first, _ = tile_state(rows)
    for place in range(rows):
        row = pl.ds(own_row(north_first, rows, place), 1)
        for k, kept in enumerate((0, 2, 3)):
            value = (top_a[k, row] + top_b[k, row]) + (top_c[k, row] + top_d[k, row])
            surface[kept, NSUB + place] = value
        surface[1, NSUB + place] = jnp.tanh(surface[0, NSUB + place])
        surface[4, NSUB + place] = rate[row]
    for side, out in enumerate((first, second)):
        early = EARLY[side]
        for f in range(early, FIELDS):
            place = NSUB + 1 if side == 0 else last - 1
            out[(f - early) * levels : (f - early + 1) * levels] = state[0, place, f]
        start = (FIELDS - early) * levels
        out[start:] = jnp.zeros((out.shape[0] - start, out.shape[1]), F32)
        for d in range(NSUB - 1):
            place = NSUB + d if side == 0 else last - d
            for k, kept in enumerate((0, 2, 3, 4)):
                at = start + 4 * d + k
                out[at : at + 1] = surface[kept, place]


def interior_updates(state, first_d):
    rows = state.shape[1] - 2 * NSUB
    last = NSUB + rows - 1
    updates = []
    for step in range(NSUB - 1):
        for d in range(step + 1, rows // 2):
            updates += [(step, NSUB + d), (step, last - d)]
    return updates[:first_d], updates[first_d:]


def first_interior_kernel(weights, turn, valid, surface, state_in, state, total, first, second, staged, sems):
    del state_in
    last = state.shape[1] - NSUB - 1
    copies = [
        pltpu.make_async_copy(state.at[0, NSUB + 2], first, sems.at[0]),
        pltpu.make_async_copy(state.at[0, last - 2], second, sems.at[1]),
    ]
    for copy in copies:
        copy.start()
    total[...] = jnp.zeros_like(total)
    updates, _ = interior_updates(state, AHEAD)
    advance(state, surface, total, weights, staged, turn, valid, updates)
    for copy in copies:
        copy.wait()


def interior_kernel(weights, turn, valid, surface, near, state_in, total_in, state, total, staged):
    del state_in, total_in
    take_rows(1, state, valid, (lambda f: near[f],))
    _, updates = interior_updates(state, AHEAD)
    advance(state, surface, total, weights, staged, turn, valid, updates)


def take_rows(number, state, valid, row_of, sides=(0, 1)):
    places = state.shape[1]
    for side, row in zip(sides, row_of):
        place = NSUB - number if side == 0 else places - 1 - NSUB + number
        for f in range(FIELDS):
            state[0, place, f] = valid[place] * row(f)


def rows_from(near, far):
    return (lambda f: near[f], lambda f: far[f])


def chain_step(number, step, state):
    low = NSUB + step + 1 - number
    return [(step, low), (step, state.shape[1] - 1 - low)]


def first_chain_kernel(weights, turn, valid, surface, far, state_in, total_in, state, total, staged):
    del state_in, total_in
    take_rows(1, state, valid, (lambda f: far[f],), (1,))
    updates = []
    for step in range(NSUB):
        updates += chain_step(1, step, state)
    advance(state, surface, total, weights, staged, turn, valid, updates)


def second_chain_kernel(weights, turn, valid, near, far, near_rest, far_rest, surface_in, state_in, total_in,
                        surface, state, total, first, second, staged, sems):
    del surface_in, state_in, total_in
    places, levels = state.shape[1], state.shape[3]
    rest = (near_rest, far_rest)
    copies = [
        pltpu.make_async_copy(state.at[0, NSUB + 3], first, sems.at[0]),
        pltpu.make_async_copy(state.at[0, places - NSUB - 4], second, sems.at[1]),
    ]
    for copy in copies:
        copy.start()

    def row_of(side, f):
        early = EARLY[side]
        if f < early:
            return (near, far)[side][FIELDS + f]
        return rest[side][(f - early) * levels : (f - early + 1) * levels]

    take_rows(2, state, valid, [functools.partial(row_of, side) for side in range(2)])
    for side in range(2):
        for d in range(NSUB - 1):
            place = NSUB - 1 - d if side == 0 else places - NSUB + d
            for k, kept in enumerate((0, 2, 3, 4)):
                at = (FIELDS - EARLY[side]) * levels + 4 * d + k
                surface[kept, place] = rest[side][at : at + 1]
            surface[1, place] = jnp.tanh(surface[0, place])
    updates = []
    for step in range(NSUB - 1):
        updates += chain_step(2, step, state)
    advance(state, surface, total, weights, staged, turn, valid, updates)
    for copy in copies:
        copy.wait()


def third_chain_kernel(weights, turn, valid, surface, near, far, state_in, total_in, state, total, flux, staged):
    del state_in, total_in
    rows = state.shape[1] - 2 * NSUB
    north_first, _ = tile_state(rows)
    take_rows(3, state, valid, rows_from(near, far))
    updates = []
    for step in range(NSUB - 1):
        updates += chain_step(3, step, state)
    advance(state, surface, total, weights, staged, turn, valid, updates)
    for place in range(NSUB, NSUB + rows):
        d = min(place - NSUB, NSUB + rows - 1 - place)
        last = surface_flux(state.at[NSUB - 1, place], surface, place) if d < NSUB - 1 else None
        for f in range(FIELDS):
            value = total[place, f] if last is None else total[place, f] + last[f]
            flux[f, pl.ds(own_row(north_first, rows, place - NSUB), 1)] = value


def finish_kernel(weights, turn, valid, surface, flux_in, state_in, state, flux, staged):
    del state_in
    flux[...] = flux_in[...]
    updates = chain_step(2, NSUB - 1, state) + chain_step(3, NSUB - 1, state)
    advance(state, surface, None, weights, staged, turn, valid, updates, False)


def send_row(state, air_next, place, sem):
    rows = air_next.shape[2]
    row = own_row(tile_state(rows)[0], rows, place)
    copy = pltpu.make_async_copy(state.at[NSUB, NSUB + place], air_next.at[0, :, row], sem)
    copy.start()
    return copy


def last_chain_kernel(weights, turn, valid, surface, near, far, state_in, state, air_next, staged, sems):
    del state_in
    rows = air_next.shape[2]
    copies = [send_row(state, air_next, place, sems.at[place]) for place in range(1, rows - 1)]
    take_rows(4, state, valid, rows_from(near, far))
    updates = []
    for step in range(NSUB):
        updates += chain_step(4, step, state)
    advance(state, surface, None, weights, staged, turn, valid, updates, False)
    for copy in copies:
        copy.wait()


def send_last_rows(state, air_next, sems):
    rows = air_next.shape[2]
    return [send_row(state, air_next, place, sems.at[k]) for k, place in enumerate((0, rows - 1))]


def last_rows_kernel(owner, state, air_in, air_next, sems):
    del air_in

    @pl.when(lax.axis_index("member") != owner[0])
    def _():
        for copy in send_last_rows(state, air_next, sems):
            copy.wait()


def sea_kernel(owner, base, column, flux_a, flux_b, flux_c, flux_d, state, sea_in, air_in, sea_next, air_next,
               result, sems, air_sems):
    del sea_in, air_in
    levels = column.shape[0]

    @pl.when(lax.axis_index("member") == owner[0])
    def _():
        copies = send_last_rows(state, air_next, air_sems)
        for f in range(FIELDS):
            mean = (flux_a[f] + flux_b[f]) + (flux_c[f] + flux_d[f])
            for h in range(base.shape[1]):
                part = mean[:, h * LANES : (h + 1) * LANES]
                for level in range(levels):
                    result[f, h, level] = base[f, h, level] + column[level] * part
                place = sea_next.at[0, f, :, :, pl.ds(h * LANES, LANES)]
                copies.append(pltpu.make_async_copy(result.at[f, h], place, sems.at[f, h]))
                copies[-1].start()
        for copy in copies:
            copy.wait()


def pairings(members, tiles):
    both = []
    for side in range(2):
        pairs = []
        for member in range(members):
            for tile in range(tiles):
                other = tile + 1 if (tile + side) % 2 == 0 else tile - 1
                if 0 <= other < tiles:
                    to = member * tiles + other
                else:
                    to = (member ^ 1) * tiles + tile
                pairs.append((member * tiles + tile, to))
        both.append(pairs)
    return both


def params(**more):
    return pltpu.CompilerParams(vmem_limit_bytes=VMEM_LIMIT, **more)


def cost(microseconds):
    return pl.CostEstimate(flops=0, bytes_accessed=int(microseconds * 3.5e6), transcendentals=0)


def exchange(values, swaps):
    return [lax.ppermute(value, AXES, swap) for value, swap in zip(values, swaps)]


def swapped(values, k):
    count = lax.axis_size("member")
    return lax.ppermute(values, "member", [(i, i ^ k) for i in range(count)])


def member_parts(values, then=None, order=1):
    k = 1
    while lax.axis_size("member") > 4 * k:
        other = swapped(values, k)
        values = (values if then is None or k > 1 else then(values)) + other
        k *= 2
    others = list(range(k, lax.axis_size("member"), k))[::order]
    return [values] + [swapped(values, other) for other in others]


def shards(
    atmos_state, ocean_slots, owner_map, land_mask, transfer_coefficient, air_mixing, sea_mixing
):
    members, tiles = lax.axis_size("member"), lax.axis_size("tile")
    _, _, rows, levels, lon = atmos_state.shape
    sea_levels = ocean_slots.shape[3]
    places = rows + 2 * NSUB
    depth, sea_depth = ceil_to(levels, 16), ceil_to(sea_levels, 16)
    swaps = pairings(members, tiles)
    sea_slots = jnp.swapaxes(ocean_slots, 2, 3)

    def rows_of(*count):
        return jax.ShapeDtypeStruct((*count, FIELDS, levels, lon), F32)

    halves, held = lon // LANES, ceil_to(sea_levels, 8)
    state_type = pltpu.VMEM((NSUB + 1, places, FIELDS, levels, lon), F32)
    surface_type = pltpu.VMEM((5, places, 1, lon), F32)
    total_type = pltpu.VMEM((places, FIELDS, 1, lon), F32)
    table_type = pltpu.VMEM((places, 1, lon), F32)
    base_type = pltpu.VMEM((FIELDS, halves, held, rows, LANES), F32)
    column_type = pltpu.VMEM((sea_levels, rows, LANES), F32)
    sea_weight_type = pltpu.VMEM((held, 3 * sea_depth), BF16)
    cell_type = pltpu.VMEM((rows, lon), F32)
    top_type = pltpu.VMEM((3, rows, lon), F32)
    flux_type = pltpu.VMEM((FIELDS, rows, lon), F32)
    air_type, sea_type = pltpu.HBM(atmos_state.shape, F32), pltpu.HBM(sea_slots.shape, F32)
    topped = [
        pltpu.VMEM((ceil_to((FIELDS - early) * levels + 4 * (NSUB - 1), 8), lon), F32) for early in EARLY
    ]
    near_types = [jax.ShapeDtypeStruct((FIELDS + early, levels, lon), F32) for early in EARLY]
    staged = pltpu.VMEM((2, FIELDS, 3 * depth, lon), BF16)
    atmos_state, sea_slots, land_cells, transfer, air_square, sea_square = [
        pltpu.with_memory_space_constraint(value, pltpu.HBM)
        for value in (
            atmos_state, sea_slots, land_mask, transfer_coefficient, air_mixing, sea_mixing
        )
    ]

    near, far, top = pl.pallas_call(
        pack_kernel,
        name="pack_rows",
        cost_estimate=cost(1),
        out_shape=(*near_types, top_type),
        in_specs=[ANY, ANY],
        out_specs=(ANY, ANY, VMEM),
        scratch_shapes=[pltpu.SemaphoreType.DMA((4,)), pltpu.SemaphoreType.DMA((3,))],
        compiler_params=params(),
    )(atmos_state, sea_slots)
    top = pl.pallas_call(
        owner_kernel,
        name="owner_surface",
        cost_estimate=cost(0.1),
        out_shape=top_type,
        in_specs=[SMEM, VMEM],
        out_specs=VMEM,
        compiler_params=params(),
    )(owner_map, top)
    arrived = exchange((near, far), swaps)
    base, sea_weights, column, land = None, None, None, None

    def sea_tables(top):
        nonlocal base, sea_weights, column, land
        base, sea_weights, column, land, again = pl.pallas_call(
            functools.partial(sea_tables_kernel, SEA_STEP / (NSUB * members)),
            name="sea_tables",
            cost_estimate=cost(1),
            out_shape=(base_type, sea_weight_type, column_type, cell_type, top_type),
            in_specs=[SMEM, ANY, ANY, ANY, VMEM],
            out_specs=(VMEM,) * 5,
            scratch_shapes=[
                pltpu.VMEM((rows, lon), jnp.int32),
                pltpu.VMEM(sea_mixing.shape, F32),
                pltpu.SemaphoreType.DMA((halves,)),
                pltpu.SemaphoreType.DMA((2,)),
            ],
            compiler_params=params(),
        )(owner_map, sea_slots, land_cells, sea_square, top)
        return again

    top_parts = member_parts(top, sea_tables, -1)

    base, sea_next = pl.pallas_call(
        ocean_kernel,
        name="ocean",
        cost_estimate=cost(1.2),
        out_shape=(base_type, sea_type),
        in_specs=[SMEM] + [VMEM] * 3,
        out_specs=(VMEM, ANY),
        input_output_aliases={3: 0},
        scratch_shapes=[
            pltpu.VMEM((2 * FIELDS, 3 * sea_depth, lon), BF16),
            pltpu.SemaphoreType.DMA((halves,)),
        ],
        compiler_params=params(),
    )(owner_map, land, sea_weights, base)

    state, weights, turn, valid, rate = pl.pallas_call(
        functools.partial(tables_kernel, rows * tiles),
        name="tables",
        cost_estimate=cost(1.5),
        out_shape=(
            state_type,
            pltpu.VMEM((3, ceil_to(levels, 8), 3 * depth), BF16),
            table_type,
            table_type,
            cell_type,
        ),
        in_specs=[ANY] * 3 + [VMEM] * 2,
        out_specs=(VMEM,) * 5,
        scratch_shapes=[
            pltpu.VMEM((rows, lon), F32),
            pltpu.VMEM(air_mixing.shape, F32),
            pltpu.SemaphoreType.DMA((rows,)),
            pltpu.SemaphoreType.DMA((2,)),
        ],
        compiler_params=params(),
    )(atmos_state, transfer, air_square, land, base)
    tables = (weights, turn, valid)

    surface, *rest_rows = pl.pallas_call(
        surface_kernel,
        name="surface",
        cost_estimate=cost(0.3),
        out_shape=(surface_type, *topped),
        in_specs=[VMEM] * 6,
        out_specs=(VMEM,) * 3,
        compiler_params=params(),
    )(*top_parts, rate, state)
    arrived_rest = exchange(rest_rows, swaps)

    state, total, *third_rows = pl.pallas_call(
        first_interior_kernel,
        name="first_interior",
        cost_estimate=cost(0.5),
        out_shape=(state_type, total_type, rows_of(), rows_of()),
        in_specs=[VMEM] * 5,
        out_specs=(VMEM, VMEM, ANY, ANY),
        input_output_aliases={4: 0},
        scratch_shapes=[staged, pltpu.SemaphoreType.DMA((2,))],
        compiler_params=params(),
    )(*tables, surface, state)
    arrived_third = exchange(third_rows, swaps)

    state, total = pl.pallas_call(
        interior_kernel,
        name="interior",
        cost_estimate=cost(2.5),
        out_shape=(state_type, total_type),
        in_specs=[VMEM] * 7,
        out_specs=(VMEM, VMEM),
        input_output_aliases={5: 0, 6: 1},
        scratch_shapes=[staged],
        compiler_params=params(),
    )(*tables, surface, arrived[0], state, total)

    state, total = pl.pallas_call(
        first_chain_kernel,
        name="first_chain",
        cost_estimate=cost(2),
        out_shape=(state_type, total_type),
        in_specs=[VMEM] * 7,
        out_specs=(VMEM, VMEM),
        input_output_aliases={5: 0, 6: 1},
        scratch_shapes=[staged],
        compiler_params=params(),
    )(*tables, surface, arrived[1], state, total)

    surface, state, total, *fourth_rows = pl.pallas_call(
        second_chain_kernel,
        name="second_chain",
        cost_estimate=cost(1.5),
        out_shape=(surface_type, state_type, total_type, rows_of(), rows_of()),
        in_specs=[VMEM] * 10,
        out_specs=(VMEM, VMEM, VMEM, ANY, ANY),
        input_output_aliases={7: 0, 8: 1, 9: 2},
        scratch_shapes=[staged, pltpu.SemaphoreType.DMA((2,))],
        compiler_params=params(),
    )(*tables, *arrived, *arrived_rest, surface, state, total)
    arrived_fourth = exchange(fourth_rows, swaps)

    state, _, flux = pl.pallas_call(
        third_chain_kernel,
        name="third_chain",
        cost_estimate=cost(1.5),
        out_shape=(state_type, total_type, flux_type),
        in_specs=[VMEM] * 8,
        out_specs=(VMEM,) * 3,
        input_output_aliases={6: 0, 7: 1},
        scratch_shapes=[staged],
        compiler_params=params(),
    )(*tables, surface, *arrived_third, state, total)

    def finish(flux):
        nonlocal state
        state, again = pl.pallas_call(
            finish_kernel,
            name="finish",
            cost_estimate=cost(1),
            out_shape=(state_type, flux_type),
            in_specs=[VMEM] * 6,
            out_specs=(VMEM, VMEM),
            input_output_aliases={5: 0},
            scratch_shapes=[staged],
            compiler_params=params(),
        )(*tables, surface, flux, state)
        return again

    flux_parts = member_parts(flux, finish, -1)

    state, air_next = pl.pallas_call(
        last_chain_kernel,
        name="last_chain",
        cost_estimate=cost(2.5),
        out_shape=(state_type, air_type),
        in_specs=[VMEM] * 7,
        out_specs=(VMEM, ANY),
        input_output_aliases={6: 0},
        scratch_shapes=[staged, pltpu.SemaphoreType.DMA((rows,))],
        compiler_params=params(),
    )(*tables, surface, *arrived_fourth, state)

    air_next = pl.pallas_call(
        last_rows_kernel,
        name="last_rows",
        cost_estimate=cost(0.6),
        out_shape=air_type,
        in_specs=[SMEM, VMEM, ANY],
        out_specs=ANY,
        input_output_aliases={2: 0},
        scratch_shapes=[pltpu.SemaphoreType.DMA((2,))],
        compiler_params=params(),
    )(owner_map, state, air_next)

    sea_next, air_next = pl.pallas_call(
        sea_kernel,
        name="sea_step",
        cost_estimate=cost(1.5),
        out_shape=(sea_type, air_type),
        in_specs=[SMEM] + [VMEM] * 7 + [ANY, ANY],
        out_specs=(ANY, ANY),
        input_output_aliases={8: 0, 9: 1},
        scratch_shapes=[
            pltpu.VMEM((FIELDS, halves, sea_levels, rows, LANES), F32),
            pltpu.SemaphoreType.DMA((FIELDS, halves)),
            pltpu.SemaphoreType.DMA((2,)),
        ],
        compiler_params=params(),
    )(owner_map, base, column, *flux_parts, state, sea_next, air_next)
    return (air_next, jnp.swapaxes(sea_next, 2, 3))


def solution(mesh):
    placed = (
        P("member", None, "tile", None, None),
        P("member", None, "tile", None, None),
        P("tile"),
        P("tile", None),
        P("tile", None),
        P(),
        P(),
    )
    return jax.shard_map(
        shards,
        mesh=mesh,
        in_specs=placed,
        out_specs=(P("member", None, "tile", None, None), P("member", None, "tile", None, None)),
        check_vma=False,
    )
```

```python
import functools
import math

import jax
import jax.numpy as jnp
from jax import lax
from jax.experimental import pallas as pl
from jax.experimental.pallas import tpu as pltpu
from jax.sharding import PartitionSpec as P

NSUB = 4
DIFFUSE = 0.2
ADVECT_RATE = 0.15
CORIOLIS_MAX = 0.2
AIR_STEP = 0.05
SEA_STEP = 0.25
SIGNS = (1.0, 1.0, -1.0, -1.0)
FIELDS = 4
LANES = 128
AHEAD = 6
EARLY = (3, 3)

F32 = jnp.float32
BF16 = jnp.bfloat16
AXES = ("member", "tile")
VMEM = pl.BlockSpec(memory_space=pltpu.VMEM)
SMEM = pl.BlockSpec(memory_space=pltpu.SMEM)
ANY = pl.BlockSpec(memory_space=pl.ANY)
VMEM_LIMIT = 12 * 2**20


def ceil_to(count, unit):
    return -(-count // unit) * unit


def split_parts(values):
    high = values.astype(BF16).astype(F32)
    return high, (values - high).astype(BF16).astype(F32)


def mixing_parts(mixing, scale):
    levels = mixing.shape[0]
    rows = lax.broadcasted_iota(jnp.int32, mixing.shape, 0)
    columns = lax.broadcasted_iota(jnp.int32, mixing.shape, 1)
    both = scale * mixing + jnp.where(rows == columns, scale, 0.0)
    extra = ceil_to(levels, 8) - levels
    if extra:
        both = jnp.concatenate([both, jnp.zeros((extra, levels), F32)], axis=0)
    high, low = split_parts(both)
    pad = jnp.zeros((both.shape[0], ceil_to(levels, 16) - levels), F32)
    parts = [high, pad, high, pad, low, pad] if pad.shape[1] else [high, high, low]
    return jnp.concatenate(parts, axis=1).astype(BF16)


def stage(cells, staged, offset, depth):
    count, lon = cells.shape
    if count < 16:
        cells = jnp.concatenate([cells, jnp.zeros((16 - count, lon), F32)], axis=0)
    high = cells.astype(BF16)
    low = (cells - high.astype(F32)).astype(BF16)
    staged[offset : offset + 16] = high
    staged[depth + offset : depth + offset + 16] = low
    staged[2 * depth + offset : 2 * depth + offset + 16] = high


def stage_dynamics(center, outer, inner, sign, coriolis, staged):
    levels, lon = center.shape[1:]
    depth = ceil_to(levels, 16)
    rate = 0.5 * ADVECT_RATE / DIFFUSE
    for offset in range(0, levels, 16):
        part = slice(offset, min(offset + 16, levels))
        cells = [center[f, part] for f in range(FIELDS)]
        east_wind = rate * cells[2]
        north_wind = (rate * sign) * cells[3]
        for f in range(FIELDS):
            outer_row, inner_row = outer[f, part], inner[f, part]
            east = pltpu.roll(cells[f], lon - 1, 1)
            west = pltpu.roll(cells[f], 1, 1)
            total = ((east + west) + (outer_row + inner_row)) + cells[f]
            if f < 2:
                total = total - (east_wind * (east - west) + north_wind * (outer_row - inner_row))
            elif f == 2:
                total = total + coriolis * cells[3]
            else:
                total = total - coriolis * cells[2]
            stage(total, staged.at[f], offset, depth)


def surface_flux(center, surface, place):
    sst, sst_tanh, cur_east, cur_north, rate = [surface[k, place] for k in range(5)]
    east = center[2, 0:1] - cur_east
    north = center[3, 0:1] - cur_north
    factor = rate * jnp.sqrt(1.0 + east * east + north * north)
    return (
        factor * (sst - center[0, 0:1]),
        factor * (sst_tanh - center[1, 0:1]),
        factor * east,
        factor * north,
    )


def tile_state(rows):
    tile = lax.axis_index("tile")
    return lax.rem(tile, 2) == 0, tile * rows


def own_row(north_first, rows, place):
    return jnp.where(north_first, rows - 1 - place, place)


def advance(state, surface, total, weights, staged, turn, valid, updates, count_flux=True):
    places = state.shape[1]
    rows = places - 2 * NSUB
    sign = jnp.where(tile_state(rows)[0], 1.0, -1.0)
    for k, (step, place) in enumerate(updates):
        slot = staged.at[k % staged.shape[0]]
        center, outer, inner = [state.at[step, place + shift] for shift in (0, -1, 1)]
        target = state.at[step + 1, place]
        stage_dynamics(center, outer, inner, sign, turn[place], slot)
        flux = surface_flux(center, surface, place)
        own = NSUB <= place < NSUB + rows
        kind = 0 if own else 1 if place < NSUB else 2
        for f in range(FIELDS):
            if own and count_flux:
                total[place, f] = total[place, f] + flux[f]
            mixed = jnp.dot(weights[kind], slot[f], preferred_element_type=F32)
            added = (AIR_STEP * SIGNS[f]) * flux[f]
            target[f] = mixed
            target[f, 0:1] = mixed[0:1] + (added if own else valid[place] * added)


def pack_kernel(air, sea, first, second, top, sems, top_sems):
    rows = air.shape[2]
    north_first, _ = tile_state(rows)
    copies = []
    for d in range(2):
        for side, out in enumerate((first, second)):
            fields = FIELDS if d == 0 else EARLY[side]
            row = own_row(north_first, rows, d if side == 0 else rows - 1 - d)
            copies.append(
                pltpu.make_async_copy(
                    air.at[0, pl.ds(0, fields), row],
                    out.at[pl.ds(d * FIELDS, fields)],
                    sems.at[2 * d + side],
                )
            )
    tops = [
        pltpu.make_async_copy(sea.at[0, f, 0], top.at[k], top_sems.at[k])
        for k, f in enumerate((0, 2, 3))
    ]
    for copy in copies + tops:
        copy.start()
    for copy in copies + tops:
        copy.wait()


def owner_kernel(owner, top, other, owned_top):
    member = lax.axis_index("member")
    here = jnp.where(owner[0] == member, top[...], 0.0)
    owned_top[...] = here + jnp.where(owner[0] == member + 1 - 2 * lax.rem(member, 2), other[...], 0.0)


def sea_tables_kernel(scale, owner, sea, land_in, sea_mixing_in, base, sea_weights, column, land,
                      land_here, sea_mixing, sems, small_sems):
    rows, levels = land.shape[0], sea.shape[2]
    held, halves = base.shape[2], base.shape[1]
    small = [
        pltpu.make_async_copy(source, here, small_sems.at[k])
        for k, (source, here) in enumerate(((sea_mixing_in, sea_mixing), (land_in, land_here)))
    ]
    loads = [
        pltpu.make_async_copy(
            sea.at[0, :, :, :, pl.ds(h * LANES, LANES)],
            base.at[:, h, pl.ds(0, levels)],
            sems.at[h],
        )
        for h in range(halves)
    ]
    for copy in small + loads:
        copy.start()
    if held > levels:
        base[:, :, levels:] = jnp.zeros((FIELDS, halves, held - levels, rows, LANES), F32)
    for copy in small:
        copy.wait()
    land[...] = land_here[...].astype(F32)
    sea_weights[...] = mixing_parts(sea_mixing[...], 0.5)
    factor = jnp.where(lax.axis_index("member") == owner[0], 0.5 * scale, 0.0)
    first_column = jnp.broadcast_to(sea_mixing[:, 0:1], (levels, LANES))
    for level in range(levels):
        value = first_column[level : level + 1] + (1.0 if level == 0 else 0.0)
        column[level] = factor * jnp.broadcast_to(value, (rows, LANES))
    for copy in loads:
        copy.wait()


def tables_kernel(row_total, air, transfer, air_mixing_in, land, after, state, weights, turn, valid, rate,
                  transfer_here, air_mixing, sems, small_sems):
    del after
    rows, lon = air.shape[2], air.shape[4]
    halves, places = lon // LANES, rows + 2 * NSUB
    north_first, first_row = tile_state(rows)
    small = [
        pltpu.make_async_copy(source, here, small_sems.at[k])
        for k, (source, here) in enumerate(((air_mixing_in, air_mixing), (transfer, transfer_here)))
    ]
    copies = []
    for place in range(rows):
        row = own_row(north_first, rows, place)
        copies.append(
            pltpu.make_async_copy(air.at[0, :, row], state.at[0, NSUB + place], sems.at[place])
        )
    for copy in small + copies:
        copy.start()
    line = lax.broadcasted_iota(jnp.int32, (places, LANES), 0) - NSUB
    index = first_row + jnp.where(north_first, rows - 1 - line, line)
    latitude = math.pi * ((index.astype(F32) + 0.5) / row_total - 0.5)
    turned = (CORIOLIS_MAX / DIFFUSE) * jnp.sin(latitude)
    inside = jnp.where((index >= 0) & (index < row_total), 1.0, 0.0)
    for place in range(places):
        part = slice(place, place + 1)
        turn[place] = jnp.concatenate([turned[part]] * halves, axis=1)
        valid[place] = jnp.concatenate([inside[part]] * halves, axis=1)
    for copy in small:
        copy.wait()
    parts = mixing_parts(air_mixing[...], 0.5 * DIFFUSE)
    weights[0] = parts
    for side, place in enumerate((NSUB - 1, NSUB + rows)):
        exists = valid[place, 0:1, 0:1].astype(BF16)
        weights[1 + side] = parts * exists
    rate[...] = transfer_here[...] * land[...]
    for copy in copies:
        copy.wait()


def ocean_kernel(part_number, owner, land, sea_weights, base_in, after, base, staged):
    del base_in, after
    held, halves, rows = base.shape[2], base.shape[1], base.shape[3]
    depth = staged.shape[1] // 3
    half = FIELDS // 2
    fields = range(part_number * half, (part_number + 1) * half)

    @pl.when(lax.axis_index("member") == owner[0])
    def _():
        flat = base.reshape(FIELDS, halves, held * rows, LANES)

        for row in range(rows):
            own = pl.ds(row, held, stride=rows)
            at_sea = land[row : row + 1] == 1.0
            for f in fields:
                slot = staged.at[(row * FIELDS + f) % staged.shape[0]]
                cells = jnp.concatenate([flat[f, h, own] for h in range(halves)], axis=1)
                for offset in range(0, held, 16):
                    part = slice(offset, min(offset + 16, held))
                    stage(cells[part], slot, offset, depth)
                mixed = jnp.dot(sea_weights[...], slot[...], preferred_element_type=F32)
                kept = jnp.where(at_sea, mixed, cells)
                for h in range(halves):
                    flat[f, h, own] = kept[:, h * LANES : (h + 1) * LANES]


def surface_kernel(top_a, top_b, top_c, top_d, rate, state, surface, first, second):
    levels = state.shape[3]
    rows = rate.shape[0]
    last = NSUB + rows - 1
    north_first, _ = tile_state(rows)
    for place in range(rows):
        row = pl.ds(own_row(north_first, rows, place), 1)
        for k, kept in enumerate((0, 2, 3)):
            value = (top_a[k, row] + top_b[k, row]) + (top_c[k, row] + top_d[k, row])
            surface[kept, NSUB + place] = value
        surface[1, NSUB + place] = jnp.tanh(surface[0, NSUB + place])
        surface[4, NSUB + place] = rate[row]
    for side, out in enumerate((first, second)):
        early = EARLY[side]
        for f in range(early, FIELDS):
            place = NSUB + 1 if side == 0 else last - 1
            out[(f - early) * levels : (f - early + 1) * levels] = state[0, place, f]
        start = (FIELDS - early) * levels
        out[start:] = jnp.zeros((out.shape[0] - start, out.shape[1]), F32)
        for d in range(NSUB - 1):
            place = NSUB + d if side == 0 else last - d
            for k, kept in enumerate((0, 2, 3, 4)):
                at = start + 4 * d + k
                out[at : at + 1] = surface[kept, place]


def interior_updates(state, first_d):
    rows = state.shape[1] - 2 * NSUB
    last = NSUB + rows - 1
    updates = []
    for step in range(NSUB - 1):
        for d in range(step + 1, rows // 2):
            updates += [(step, NSUB + d), (step, last - d)]
    return updates[:first_d], updates[first_d:]


def first_interior_kernel(weights, turn, valid, surface, state_in, state, total, first, second, staged, sems):
    del state_in
    last = state.shape[1] - NSUB - 1
    copies = [
        pltpu.make_async_copy(state.at[0, NSUB + 2], first, sems.at[0]),
        pltpu.make_async_copy(state.at[0, last - 2], second, sems.at[1]),
    ]
    for copy in copies:
        copy.start()
    total[...] = jnp.zeros_like(total)
    updates, _ = interior_updates(state, AHEAD)
    advance(state, surface, total, weights, staged, turn, valid, updates)
    for copy in copies:
        copy.wait()


def interior_kernel(weights, turn, valid, surface, near, state_in, total_in, state, total, staged):
    del state_in, total_in
    take_rows(1, state, valid, (lambda f: near[f],))
    _, updates = interior_updates(state, AHEAD)
    advance(state, surface, total, weights, staged, turn, valid, updates)


def take_rows(number, state, valid, row_of, sides=(0, 1)):
    places = state.shape[1]
    for side, row in zip(sides, row_of):
        place = NSUB - number if side == 0 else places - 1 - NSUB + number
        for f in range(FIELDS):
            state[0, place, f] = valid[place] * row(f)


def rows_from(near, far):
    return (lambda f: near[f], lambda f: far[f])


def chain_step(number, step, state):
    low = NSUB + step + 1 - number
    return [(step, low), (step, state.shape[1] - 1 - low)]


def first_chain_kernel(weights, turn, valid, surface, far, state_in, total_in, state, total, staged):
    del state_in, total_in
    take_rows(1, state, valid, (lambda f: far[f],), (1,))
    updates = []
    for step in range(NSUB):
        updates += chain_step(1, step, state)
    advance(state, surface, total, weights, staged, turn, valid, updates)


def second_chain_kernel(weights, turn, valid, near, far, near_rest, far_rest, surface_in, state_in, total_in,
                        surface, state, total, first, second, staged, sems):
    del surface_in, state_in, total_in
    places, levels = state.shape[1], state.shape[3]
    rest = (near_rest, far_rest)
    copies = [
        pltpu.make_async_copy(state.at[0, NSUB + 3], first, sems.at[0]),
        pltpu.make_async_copy(state.at[0, places - NSUB - 4], second, sems.at[1]),
    ]
    for copy in copies:
        copy.start()

    def row_of(side, f):
        early = EARLY[side]
        if f < early:
            return (near, far)[side][FIELDS + f]
        return rest[side][(f - early) * levels : (f - early + 1) * levels]

    take_rows(2, state, valid, [functools.partial(row_of, side) for side in range(2)])
    for side in range(2):
        for d in range(NSUB - 1):
            place = NSUB - 1 - d if side == 0 else places - NSUB + d
            for k, kept in enumerate((0, 2, 3, 4)):
                at = (FIELDS - EARLY[side]) * levels + 4 * d + k
                surface[kept, place] = rest[side][at : at + 1]
            surface[1, place] = jnp.tanh(surface[0, place])
    updates = []
    for step in range(NSUB - 1):
        updates += chain_step(2, step, state)
    advance(state, surface, total, weights, staged, turn, valid, updates)
    for copy in copies:
        copy.wait()


def third_chain_kernel(weights, turn, valid, surface, near, far, state_in, total_in, after, state, total, flux,
                       staged):
    del state_in, total_in, after
    rows = state.shape[1] - 2 * NSUB
    north_first, _ = tile_state(rows)
    take_rows(3, state, valid, rows_from(near, far))
    updates = []
    for step in range(NSUB - 1):
        updates += chain_step(3, step, state)
    advance(state, surface, total, weights, staged, turn, valid, updates)
    for place in range(NSUB, NSUB + rows):
        d = min(place - NSUB, NSUB + rows - 1 - place)
        last = surface_flux(state.at[NSUB - 1, place], surface, place) if d < NSUB - 1 else None
        for f in range(FIELDS):
            value = total[place, f] if last is None else total[place, f] + last[f]
            flux[f, pl.ds(own_row(north_first, rows, place - NSUB), 1)] = value


def finish_kernel(weights, turn, valid, surface, flux_in, state_in, state, flux, staged):
    del state_in
    flux[...] = flux_in[...]
    updates = chain_step(2, NSUB - 1, state) + chain_step(3, NSUB - 1, state)
    advance(state, surface, None, weights, staged, turn, valid, updates, False)


def send_row(state, air_next, place, sem):
    rows = air_next.shape[2]
    row = own_row(tile_state(rows)[0], rows, place)
    copy = pltpu.make_async_copy(state.at[NSUB, NSUB + place], air_next.at[0, :, row], sem)
    copy.start()
    return copy


def last_chain_kernel(owner, weights, turn, valid, surface, near, far, base, state_in, state, air_next, sea_next,
                      staged, sems, sea_sems):
    del state_in
    levels = sea_next.shape[2]
    stores = [
        pltpu.make_async_copy(
            base.at[:, h, pl.ds(0, levels)],
            sea_next.at[0, :, :, :, pl.ds(h * LANES, LANES)],
            sea_sems.at[h],
        )
        for h in range(base.shape[1])
    ]
    others = lax.axis_index("member") != owner[0]

    @pl.when(others)
    def _():
        for store in stores:
            store.start()

    rows = air_next.shape[2]
    copies = [send_row(state, air_next, place, sems.at[place]) for place in range(1, rows - 1)]
    take_rows(4, state, valid, rows_from(near, far))
    updates = []
    for step in range(NSUB):
        updates += chain_step(4, step, state)
    advance(state, surface, None, weights, staged, turn, valid, updates, False)
    for copy in copies:
        copy.wait()

    @pl.when(others)
    def _():
        for store in stores:
            store.wait()


def send_last_rows(state, air_next, sems):
    rows = air_next.shape[2]
    return [send_row(state, air_next, place, sems.at[k]) for k, place in enumerate((0, rows - 1))]


def last_rows_kernel(owner, state, air_in, air_next, sems):
    del air_in

    @pl.when(lax.axis_index("member") != owner[0])
    def _():
        for copy in send_last_rows(state, air_next, sems):
            copy.wait()


def sea_kernel(owner, base, column, flux_a, flux_b, flux_c, flux_d, state, sea_in, air_in, sea_next, air_next,
               result, sems, air_sems):
    del sea_in, air_in
    levels = column.shape[0]

    @pl.when(lax.axis_index("member") == owner[0])
    def _():
        copies = send_last_rows(state, air_next, air_sems)
        for f in range(FIELDS):
            mean = (flux_a[f] + flux_b[f]) + (flux_c[f] + flux_d[f])
            for h in range(base.shape[1]):
                part = mean[:, h * LANES : (h + 1) * LANES]
                for level in range(levels):
                    result[f, h, level] = base[f, h, level] + column[level] * part
                place = sea_next.at[0, f, :, :, pl.ds(h * LANES, LANES)]
                copies.append(pltpu.make_async_copy(result.at[f, h], place, sems.at[f, h]))
                copies[-1].start()
        for copy in copies:
            copy.wait()


def pairings(members, tiles):
    both = []
    for side in range(2):
        pairs = []
        for member in range(members):
            for tile in range(tiles):
                other = tile + 1 if (tile + side) % 2 == 0 else tile - 1
                if 0 <= other < tiles:
                    to = member * tiles + other
                else:
                    to = (member ^ 1) * tiles + tile
                pairs.append((member * tiles + tile, to))
        both.append(pairs)
    return both


def params(**more):
    return pltpu.CompilerParams(vmem_limit_bytes=VMEM_LIMIT, **more)


def cost(microseconds):
    return pl.CostEstimate(flops=0, bytes_accessed=int(microseconds * 3.5e6), transcendentals=0)


def exchange(values, swaps):
    return [lax.ppermute(value, AXES, swap) for value, swap in zip(values, swaps)]


def swapped(values, k):
    count = lax.axis_size("member")
    return lax.ppermute(values, "member", [(i, i ^ k) for i in range(count)])


def member_parts(values, then=None, order=1, k=1):
    while lax.axis_size("member") > 4 * k:
        other = swapped(values, k)
        values = (values if then is None or k > 1 else then(values)) + other
        k *= 2
    others = list(range(k, lax.axis_size("member"), k))[::order]
    return [values] + [swapped(values, other) for other in others]


def shards(
    atmos_state, ocean_slots, owner_map, land_mask, transfer_coefficient, air_mixing, sea_mixing
):
    members, tiles = lax.axis_size("member"), lax.axis_size("tile")
    _, _, rows, levels, lon = atmos_state.shape
    sea_levels = ocean_slots.shape[3]
    places = rows + 2 * NSUB
    depth, sea_depth = ceil_to(levels, 16), ceil_to(sea_levels, 16)
    swaps = pairings(members, tiles)
    sea_slots = jnp.swapaxes(ocean_slots, 2, 3)

    def rows_of(*count):
        return jax.ShapeDtypeStruct((*count, FIELDS, levels, lon), F32)

    halves, held = lon // LANES, ceil_to(sea_levels, 8)
    state_type = pltpu.VMEM((NSUB + 1, places, FIELDS, levels, lon), F32)
    surface_type = pltpu.VMEM((5, places, 1, lon), F32)
    total_type = pltpu.VMEM((places, FIELDS, 1, lon), F32)
    table_type = pltpu.VMEM((places, 1, lon), F32)
    base_type = pltpu.VMEM((FIELDS, halves, held, rows, LANES), F32)
    column_type = pltpu.VMEM((sea_levels, rows, LANES), F32)
    sea_weight_type = pltpu.VMEM((held, 3 * sea_depth), BF16)
    cell_type = pltpu.VMEM((rows, lon), F32)
    top_type = pltpu.VMEM((3, rows, lon), F32)
    flux_type = pltpu.VMEM((FIELDS, rows, lon), F32)
    air_type, sea_type = pltpu.HBM(atmos_state.shape, F32), pltpu.HBM(sea_slots.shape, F32)
    topped = [
        pltpu.VMEM((ceil_to((FIELDS - early) * levels + 4 * (NSUB - 1), 8), lon), F32) for early in EARLY
    ]
    near_types = [jax.ShapeDtypeStruct((FIELDS + early, levels, lon), F32) for early in EARLY]
    staged = pltpu.VMEM((2, FIELDS, 3 * depth, lon), BF16)
    atmos_state, sea_slots, land_cells, transfer, air_square, sea_square = [
        pltpu.with_memory_space_constraint(value, pltpu.HBM)
        for value in (
            atmos_state, sea_slots, land_mask, transfer_coefficient, air_mixing, sea_mixing
        )
    ]

    near, far, top = pl.pallas_call(
        pack_kernel,
        name="pack_rows",
        cost_estimate=cost(1),
        out_shape=(*near_types, top_type),
        in_specs=[ANY, ANY],
        out_specs=(ANY, ANY, VMEM),
        scratch_shapes=[pltpu.SemaphoreType.DMA((4,)), pltpu.SemaphoreType.DMA((3,))],
        compiler_params=params(),
    )(atmos_state, sea_slots)
    arrived = exchange((near, far), swaps)
    top = pl.pallas_call(
        owner_kernel,
        name="owner_surface",
        cost_estimate=cost(0.1),
        out_shape=top_type,
        in_specs=[SMEM, VMEM, VMEM],
        out_specs=VMEM,
        compiler_params=params(),
    )(owner_map, top, swapped(top, 1))
    top_parts = member_parts(top, order=-1, k=2)
    base, sea_weights, column, land = pl.pallas_call(
        functools.partial(sea_tables_kernel, SEA_STEP / (NSUB * members)),
        name="sea_tables",
        cost_estimate=cost(1.5),
        out_shape=(base_type, sea_weight_type, column_type, cell_type),
        in_specs=[SMEM, ANY, ANY, ANY],
        out_specs=(VMEM,) * 4,
        scratch_shapes=[
            pltpu.VMEM((rows, lon), jnp.int32),
            pltpu.VMEM(sea_mixing.shape, F32),
            pltpu.SemaphoreType.DMA((halves,)),
            pltpu.SemaphoreType.DMA((2,)),
        ],
        compiler_params=params(),
    )(owner_map, sea_slots, land_cells, sea_square)

    def ocean(part, base, after):
        return pl.pallas_call(
            functools.partial(ocean_kernel, part),
            name="ocean",
            cost_estimate=cost(0.6),
            out_shape=base_type,
            in_specs=[SMEM] + [VMEM] * 4,
            out_specs=VMEM,
            input_output_aliases={3: 0},
            scratch_shapes=[pltpu.VMEM((2 * FIELDS, 3 * sea_depth, lon), BF16)],
            compiler_params=params(),
        )(owner_map, land, sea_weights, base, after)

    state, weights, turn, valid, rate = pl.pallas_call(
        functools.partial(tables_kernel, rows * tiles),
        name="tables",
        cost_estimate=cost(1.5),
        out_shape=(
            state_type,
            pltpu.VMEM((3, ceil_to(levels, 8), 3 * depth), BF16),
            table_type,
            table_type,
            cell_type,
        ),
        in_specs=[ANY] * 3 + [VMEM] * 2,
        out_specs=(VMEM,) * 5,
        scratch_shapes=[
            pltpu.VMEM((rows, lon), F32),
            pltpu.VMEM(air_mixing.shape, F32),
            pltpu.SemaphoreType.DMA((rows,)),
            pltpu.SemaphoreType.DMA((2,)),
        ],
        compiler_params=params(),
    )(atmos_state, transfer, air_square, land, base)
    tables = (weights, turn, valid)

    surface, *rest_rows = pl.pallas_call(
        surface_kernel,
        name="surface",
        cost_estimate=cost(0.3),
        out_shape=(surface_type, *topped),
        in_specs=[VMEM] * 6,
        out_specs=(VMEM,) * 3,
        compiler_params=params(),
    )(*top_parts, rate, state)
    arrived_rest = exchange(rest_rows, swaps)

    state, total, *third_rows = pl.pallas_call(
        first_interior_kernel,
        name="first_interior",
        cost_estimate=cost(0.5),
        out_shape=(state_type, total_type, rows_of(), rows_of()),
        in_specs=[VMEM] * 5,
        out_specs=(VMEM, VMEM, ANY, ANY),
        input_output_aliases={4: 0},
        scratch_shapes=[staged, pltpu.SemaphoreType.DMA((2,))],
        compiler_params=params(),
    )(*tables, surface, state)
    arrived_third = exchange(third_rows, swaps)

    state, total = pl.pallas_call(
        interior_kernel,
        name="interior",
        cost_estimate=cost(2.5),
        out_shape=(state_type, total_type),
        in_specs=[VMEM] * 7,
        out_specs=(VMEM, VMEM),
        input_output_aliases={5: 0, 6: 1},
        scratch_shapes=[staged],
        compiler_params=params(),
    )(*tables, surface, arrived[0], state, total)

    state, total = pl.pallas_call(
        first_chain_kernel,
        name="first_chain",
        cost_estimate=cost(2),
        out_shape=(state_type, total_type),
        in_specs=[VMEM] * 7,
        out_specs=(VMEM, VMEM),
        input_output_aliases={5: 0, 6: 1},
        scratch_shapes=[staged],
        compiler_params=params(),
    )(*tables, surface, arrived[1], state, total)

    surface, state, total, *fourth_rows = pl.pallas_call(
        second_chain_kernel,
        name="second_chain",
        cost_estimate=cost(1.5),
        out_shape=(surface_type, state_type, total_type, rows_of(), rows_of()),
        in_specs=[VMEM] * 10,
        out_specs=(VMEM, VMEM, VMEM, ANY, ANY),
        input_output_aliases={7: 0, 8: 1, 9: 2},
        scratch_shapes=[staged, pltpu.SemaphoreType.DMA((2,))],
        compiler_params=params(),
    )(*tables, *arrived, *arrived_rest, surface, state, total)
    arrived_fourth = exchange(fourth_rows, swaps)

    base = ocean(0, base, total)

    state, _, flux = pl.pallas_call(
        third_chain_kernel,
        name="third_chain",
        cost_estimate=cost(1.5),
        out_shape=(state_type, total_type, flux_type),
        in_specs=[VMEM] * 9,
        out_specs=(VMEM,) * 3,
        input_output_aliases={6: 0, 7: 1},
        scratch_shapes=[staged],
        compiler_params=params(),
    )(*tables, surface, *arrived_third, state, total, base)

    def finish(flux):
        nonlocal state
        state, again = pl.pallas_call(
            finish_kernel,
            name="finish",
            cost_estimate=cost(1),
            out_shape=(state_type, flux_type),
            in_specs=[VMEM] * 6,
            out_specs=(VMEM, VMEM),
            input_output_aliases={5: 0},
            scratch_shapes=[staged],
            compiler_params=params(),
        )(*tables, surface, flux, state)
        return again

    flux_parts = member_parts(flux, finish, -1)

    base = ocean(1, base, state)

    state, air_next, sea_next = pl.pallas_call(
        last_chain_kernel,
        name="last_chain",
        cost_estimate=cost(2.5),
        out_shape=(state_type, air_type, sea_type),
        in_specs=[SMEM] + [VMEM] * 8,
        out_specs=(VMEM, ANY, ANY),
        input_output_aliases={8: 0},
        scratch_shapes=[
            staged,
            pltpu.SemaphoreType.DMA((rows,)),
            pltpu.SemaphoreType.DMA((halves,)),
        ],
        compiler_params=params(),
    )(owner_map, *tables, surface, *arrived_fourth, base, state)

    air_next = pl.pallas_call(
        last_rows_kernel,
        name="last_rows",
        cost_estimate=cost(0.6),
        out_shape=air_type,
        in_specs=[SMEM, VMEM, ANY],
        out_specs=ANY,
        input_output_aliases={2: 0},
        scratch_shapes=[pltpu.SemaphoreType.DMA((2,))],
        compiler_params=params(),
    )(owner_map, state, air_next)

    sea_next, air_next = pl.pallas_call(
        sea_kernel,
        name="sea_step",
        cost_estimate=cost(1.5),
        out_shape=(sea_type, air_type),
        in_specs=[SMEM] + [VMEM] * 7 + [ANY, ANY],
        out_specs=(ANY, ANY),
        input_output_aliases={8: 0, 9: 1},
        scratch_shapes=[
            pltpu.VMEM((FIELDS, halves, sea_levels, rows, LANES), F32),
            pltpu.SemaphoreType.DMA((FIELDS, halves)),
            pltpu.SemaphoreType.DMA((2,)),
        ],
        compiler_params=params(),
    )(owner_map, base, column, *flux_parts, state, sea_next, air_next)
    return (air_next, jnp.swapaxes(sea_next, 2, 3))


def solution(mesh):
    placed = (
        P("member", None, "tile", None, None),
        P("member", None, "tile", None, None),
        P("tile"),
        P("tile", None),
        P("tile", None),
        P(),
        P(),
    )
    return jax.shard_map(
        shards,
        mesh=mesh,
        in_specs=placed,
        out_specs=(P("member", None, "tile", None, None), P("member", None, "tile", None, None)),
        check_vma=False,
    )
```
